32 devices in a mesh: rep: 8 (over y, x, core), shard: 4 (over z).
Axes of the slice: x: 2, y: 2, z: 4, core: 2. Of those that a mesh axis runs over, the one named last changes fastest.
Arguments:
- tokens: bfloat16 [8192, 2048], P(('rep', 'shard')), may hold values from -11 to 11, as said below
- cotangent: bfloat16 [8192, 2048], P(('rep', 'shard')), may hold values from -6 to 6
- segment_ids: int32 [8192], P(('rep', 'shard')), may hold values from 0 to 4, as said below
- expert_ids: int32 [8192, 2], P(('rep', 'shard')), may hold values from 0 to 3, all different within a row; in each aligned block of 256 rows (0 to 255, 256 to 511, ...) at most 192 rows name the same one
- norm_gain: float32 [2048], replicated, may hold values from 0.1 to 1.9
- w_query: bfloat16 [2048, 2048], P('shard'), may hold values from -0.125 to 0.125
- w_key: bfloat16 [2048, 2048], P('shard'), may hold values from -0.125 to 0.125
- w_value: bfloat16 [2048, 2048], P('shard'), may hold values from -0.125 to 0.125
- w_output: bfloat16 [2048, 2048], P('shard'), may hold values from -1.5 to 1.5
- query_gain: float32 [128], replicated, may hold values from 0.1 to 1.9
- key_gain: float32 [128], replicated, may hold values from 0.1 to 1.9
- ffn_norm_gain: float32 [2048], replicated, may hold values from 0.1 to 1.9
- w_router: bfloat16 [2048, 4], replicated, may hold values from -0.09375 to 0.09375
- w_gate: bfloat16 [4, 2048, 1024], P(None, 'shard'), may hold values from -0.125 to 0.125
- w_up: bfloat16 [4, 2048, 1024], P(None, 'shard'), may hold values from -0.125 to 0.125
- w_down: bfloat16 [4, 1024, 2048], P(None, 'shard'), may hold values from -0.5 to 0.5
Outputs:
- output: bfloat16 [8192, 2048], P(('rep', 'shard'))
- input_grad: bfloat16 [8192, 2048], P(('rep', 'shard'))
- grad_norm_gain: float32 [2048], replicated
- grad_w_query: float32 [2048, 2048], P('shard')
- grad_w_key: float32 [2048, 2048], P('shard')
- grad_w_value: float32 [2048, 2048], P('shard')
- grad_w_output: float32 [2048, 2048], P('shard')
- grad_query_gain: float32 [128], replicated
- grad_key_gain: float32 [128], replicated
- grad_ffn_norm_gain: float32 [2048], replicated
- grad_w_router: float32 [2048, 4], replicated
- grad_w_gate: float32 [4, 2048, 1024], P(None, 'shard')
- grad_w_up: float32 [4, 2048, 1024], P(None, 'shard')
- grad_w_down: float32 [4, 1024, 2048], P(None, 'shard')
- residual_rms: float32 [3], replicated
The draws below stay inside these ranges and needn't reach their ends.
Inputs may be any that keep to these rules, and one draw needn't show every extreme that they name: Row scales differ along the tokens. `segment_ids`: in each sequence of 256 tokens the ids are 1, 2, 3, 4 in order, each document one token or more, followed by 1 to 32 padding tokens of id 0. `expert_ids`: A token's 2 experts differ. In each sequence of 256 tokens no expert is chosen by more than 192 tokens, and in some sequence one expert is chosen by exactly 192.
All inputs are finite; a program needn't handle non-finite values.
Results may differ from the reference program's by a relative error of at most 0.02.
Values may be sent and summed in bfloat16 or wider, within the bound.
No kernel may reach another device: no remote copies, remote signals or barrier semaphores. Data moves between devices by JAX's collectives and lax.ppermute only.
A program may use at most 448 MiB of HBM per device.

```python
import math
import jax
import jax.numpy as jnp
import numpy as np
from jax import lax

D = 2048
HEADS = 16
HEAD_DIM = 128
H = 1024
EXPERTS = 4
TOP = 2
TOK_DEV = 256
CAP = 192
TOKENS = 8192


def draw_tokens(key, part):
    key = jax.random.fold_in(key, 11)
    row_frac = jnp.arange(TOKENS, dtype=jnp.float32) / TOKENS
    values = jnp.clip(jax.random.normal(key, (TOKENS, D), jnp.float32), -6.0, 6.0)
    row_scale = 0.6 * 3.0 ** row_frac
    return (values * row_scale[:, None]).astype(jnp.bfloat16)


def draw_segment_ids(key, part):
    key = jax.random.fold_in(key, 23)
    sequences = TOKENS // TOK_DEV
    eighth = TOK_DEV // 8
    quarter = TOK_DEV // 4
    key_pair = jax.random.split(key, 2)
    jitter = jax.random.randint(key_pair[0], (sequences, 3), -eighth, eighth)
    cut_points = (jnp.arange(1, 4) * quarter)[None, :] + jitter
    pad_length = jax.random.randint(key_pair[1], (sequences, 1), 1, eighth + 1)
    position = jnp.arange(TOK_DEV)[None, :]
    doc_ids = 1 + jnp.sum((position[:, :, None] >= cut_points[:, None, :]).astype(jnp.int32), axis=-1)
    doc_ids = jnp.where(position >= TOK_DEV - pad_length, 0, doc_ids)
    return doc_ids.reshape(TOKENS).astype(jnp.int32)


def shard_levels(own_key, extent, pieces, smallest, largest):
    def one(dim, shards_of):
        heights = jax.random.uniform(jax.random.fold_in(jax.random.fold_in(own_key, 6), dim), (shards_of,), jnp.float32, smallest / len(pieces), largest / len(pieces))
        return jnp.repeat(jnp.exp(heights), extent[dim] // shards_of).reshape((-1,) + (1,) * (len(extent) - dim - 1))

    loudness = one(*pieces[0])
    for cut in pieces[1:]:
        loudness = loudness * one(*cut)
    return loudness


def assign_block(rng, own, number, rows, count, top, limit, slope):
    sequence = jax.random.permutation(rng, count)
    crowded, common = load_shares(count, rows * top, limit, slope, True), load_shares(count, rows * top, limit, slope, False)
    places = jnp.arange(count)

    def named(sizes, offset_by):
        used = int((sizes > 0).sum())
        fixed = max(1, used // 4)
        moved = fixed + (places - fixed + offset_by * (used - fixed)) % max(1, count - fixed)
        return jnp.zeros((count,), jnp.int32).at[sequence[jnp.where(places < fixed, places, moved)]].set(jnp.asarray(sizes, jnp.int32))

    sizes = jnp.where(number % 4 == 0, named(crowded, number // 4), named(common, number - number // 4 - 1))
    mixed = jax.random.permutation(jax.random.fold_in(own, 3), count)
    source_of, taker = mixed[0:count // 2 * 2:2], mixed[1:count // 2 * 2:2]
    slack = jnp.minimum(sizes[source_of] - 1, limit - sizes[taker]) // 2
    slack = jnp.where((source_of == sequence[0]) | (taker == sequence[0]) | (sizes[taker] == 0), 0, jnp.maximum(slack, 0))
    moved = jax.random.randint(jax.random.fold_in(own, 4), (count // 2,), 0, 1 << 20) % (slack + 1)
    sizes = sizes.at[source_of].add(-moved).at[taker].add(moved)
    items = jnp.searchsorted(jnp.cumsum(sizes), jnp.arange(rows * top), side="right").astype(jnp.int32)
    grid = items.reshape(top, rows).T
    grid = grid[jax.random.permutation(jax.random.fold_in(own, 1), rows)]
    offset_by = jax.random.randint(jax.random.fold_in(own, 2), (rows, 1), 0, top)
    return jnp.take_along_axis(grid, (jnp.arange(top)[None, :] + offset_by) % top, axis=1)


def load_shares(count, total, most, lean, full):
    weights = [(1 << 20) // math.isqrt(standing ** lean) + 1 for standing in range(1, count + 1)]
    largest = most if full else min(most, max(-(-total // count), total * weights[0] // sum(weights)))
    least = 1 if total - largest >= count - 1 else 0
    counts, spare = [largest] + [least] * (count - 1), total - largest - least * (count - 1)
    while spare > 0:
        free = [i for i in range(1, count) if counts[i] < largest] or [i for i in range(1, count) if counts[i] < most]
        mass, remaining = sum([weights[i] for i in free]), spare
        for i in free:
            extra = min(most - counts[i], max(1, remaining * weights[i] // mass), spare)
            counts[i] = counts[i] + extra
            spare = spare - extra
    return np.array(counts)


def normal_values(rng, dims, scale, most, shards=(), kind=jnp.bfloat16):
    array = jax.random.normal(rng, dims, jnp.float32) * scale
    if len(shards) > 0:
        array = shard_levels(rng, dims, shards, -0.22, 0.18) * array
    return jnp.clip(array, min=-most, max=most).astype(kind)


def setup_inputs(seed: int = 0) -> dict:
    key_list = jax.random.split(jax.random.key(seed), 17)
    tokens = draw_tokens(jax.random.fold_in(key_list[16], 71), 0)
    cotangent = normal_values(key_list[1], (TOKENS, D), 1.0, 6.0, ((0, 32),))
    segment_ids = draw_segment_ids(jax.random.fold_in(key_list[16], 71), 0)
    expert_ids_keys = jax.random.split(jax.random.fold_in(key_list[3], 1), TOKENS // TOK_DEV)
    expert_ids_turns = jax.random.permutation(jax.random.fold_in(key_list[3], 3), TOKENS // TOK_DEV)
    expert_ids = jax.vmap(lambda own, number: assign_block(jax.random.fold_in(key_list[3], 2), own, number, TOK_DEV, EXPERTS, TOP, CAP, 1))(expert_ids_keys, expert_ids_turns).reshape((TOKENS, TOP))
    norm_gain = jnp.clip(1.0 + 0.18 * jax.random.normal(key_list[4], (D,), jnp.float32), 0.1, 1.9)
    w_query = normal_values(key_list[5], (D, D), D ** -0.5, 0.125, ((0, 4),))
    w_key = normal_values(key_list[6], (D, D), D ** -0.5, 0.125, ((0, 4),))
    w_value = normal_values(key_list[7], (D, D), D ** -0.5, 0.125, ((0, 4),))
    w_output = normal_values(key_list[8], (D, D), (max(D // 128, 4)) ** -0.5, 1.5, ((0, 4),))
    query_gain = jnp.clip(1.0 + 0.18 * jax.random.normal(key_list[9], (HEAD_DIM,), jnp.float32), 0.1, 1.9)
    key_gain = jnp.clip(1.0 + 0.18 * jax.random.normal(key_list[10], (HEAD_DIM,), jnp.float32), 0.1, 1.9)
    ffn_norm_gain = jnp.clip(1.0 + 0.18 * jax.random.normal(key_list[11], (D,), jnp.float32), 0.1, 1.9)
    w_router = normal_values(key_list[12], (D, EXPERTS), (2 * D) ** -0.5, 0.09375)
    w_gate = normal_values(key_list[13], (EXPERTS, D, H), D ** -0.5, 0.125, ((1, 4),))
    w_up = normal_values(key_list[14], (EXPERTS, D, H), D ** -0.5, 0.125, ((1, 4),))
    w_down = normal_values(key_list[15], (EXPERTS, H, D), (H // 8) ** -0.5, 0.5, ((1, 4),))
    return dict(tokens=tokens, cotangent=cotangent, segment_ids=segment_ids, expert_ids=expert_ids, norm_gain=norm_gain, w_query=w_query, w_key=w_key, w_value=w_value, w_output=w_output, query_gain=query_gain, key_gain=key_gain, ffn_norm_gain=ffn_norm_gain, w_router=w_router, w_gate=w_gate, w_up=w_up, w_down=w_down)


epsilon = 1e-06
theta = 10000.0
masked_score = -1e+30

@jax.custom_vjp
def low(v):
    return lax.optimization_barrier(v.astype(jnp.bfloat16)).astype(jnp.float32)

@jax.custom_vjp
def low_back(v):
    return v

def low_keep(v):
    return (low(v), None)

def low_pass(kept, grad):
    return (grad,)

def back_keep(v):
    return (v, None)

def back_low(kept, grad):
    return (low(grad),)
low.defvjp(low_keep, low_pass)
low_back.defvjp(back_keep, back_low)

def matmul_high(left_side, right_side):
    return jnp.dot(left_side, right_side, precision=lax.Precision.HIGHEST)

def rms_norm(field, gain_vec):
    return field * lax.rsqrt(lax.optimization_barrier(jnp.mean(field * field, axis=-1, keepdims=True)) + epsilon) * gain_vec

def softmax_rows(field):
    shifted = field - lax.optimization_barrier(jnp.max(field, axis=-1, keepdims=True))
    exponent = jnp.exp(shifted)
    return exponent / lax.optimization_barrier(jnp.sum(exponent, axis=-1, keepdims=True))

def rotary_tables(length, dim_size):
    half_size = dim_size // 2
    frequency = theta ** (-2.0 * jnp.arange(half_size, dtype=jnp.float32) / dim_size)
    angles = jnp.arange(length, dtype=jnp.float32)[:, None] * frequency[None, :]
    return (jnp.cos(angles)[:, None, :], jnp.sin(angles)[:, None, :])

def rotate(field, cosine, sine_table):
    half_size = field.shape[-1] // 2
    first_half = field[..., :half_size]
    second_half = field[..., half_size:]
    return jnp.concatenate([first_half * cosine - second_half * sine_table, second_half * cosine + first_half * sine_table], axis=-1)

def block_forward(params, stream, doc_ids, routes):
    norm_gain, w_query, w_key, w_value, w_output, query_gain, key_gain, ffn_norm_gain, w_router, w_gate, w_up, w_down = params
    length = stream.shape[0]
    live_rows = (doc_ids > 0).astype(jnp.float32)[:, None]
    normed = low(rms_norm(stream, norm_gain))
    query_raw = low_back(matmul_high(normed, w_query)).reshape(length, HEADS, HEAD_DIM)
    key_raw = low_back(matmul_high(normed, w_key)).reshape(length, HEADS, HEAD_DIM)
    value_heads = low(low_back(matmul_high(normed, w_value))).reshape(length, HEADS, HEAD_DIM)
    cosine, sine_table = rotary_tables(length, HEAD_DIM)
    query_rot = low(rotate(rms_norm(query_raw, query_gain), cosine, sine_table))
    key_rot = low(rotate(rms_norm(key_raw, key_gain), cosine, sine_table))
    scores = low_back(jnp.einsum('qhd,khd->hqk', query_rot, key_rot, precision=lax.Precision.HIGHEST) * HEAD_DIM ** (-0.5))
    same_document = (doc_ids[:, None] == doc_ids[None, :])[None]
    weights_soft = low(softmax_rows(jnp.where(same_document, scores, masked_score)))
    mixed_heads = jnp.einsum('hqk,khd->qhd', weights_soft, value_heads, precision=lax.Precision.HIGHEST).reshape(length, D)
    mixed_heads = low(low_back(mixed_heads))
    hidden = stream + live_rows * low_back(matmul_high(mixed_heads, w_output))
    normed_ffn = low(rms_norm(hidden, ffn_norm_gain))
    chances = softmax_rows(low_back(matmul_high(normed_ffn, w_router)))
    chosen = routes[:, :, None] == jnp.arange(EXPERTS)[None, None, :]
    combine = lax.optimization_barrier(jnp.sum(jnp.where(chosen, chances[:, None, :], 0.0), axis=1))
    gate_pre = low_back(jnp.einsum('td,edh->eth', normed_ffn, w_gate, precision=lax.Precision.HIGHEST))
    up_pre = low_back(jnp.einsum('td,edh->eth', normed_ffn, w_up, precision=lax.Precision.HIGHEST))
    inner_act = low(jax.nn.silu(gate_pre) * up_pre)
    expert_out = low_back(jnp.einsum('eth,ehd->etd', inner_act, w_down, precision=lax.Precision.HIGHEST))
    moe_out = jnp.einsum('te,etd->td', combine, expert_out, precision=lax.Precision.HIGHEST)
    return (hidden + live_rows * moe_out, hidden)

def reference(tokens, cotangent, segment_ids, expert_ids, norm_gain, w_query, w_key, w_value, w_output, query_gain, key_gain, ffn_norm_gain, w_router, w_gate, w_up, w_down):
    params = tuple((tensor.astype(jnp.float32) for tensor in (norm_gain, w_query, w_key, w_value, w_output, query_gain, key_gain, ffn_norm_gain, w_router, w_gate, w_up, w_down)))
    sequences = tokens.shape[0] // TOK_DEV
    stream = tokens.astype(jnp.float32).reshape(sequences, TOK_DEV, D)
    doc_ids = segment_ids.reshape(sequences, TOK_DEV)
    routes = expert_ids.reshape(sequences, TOK_DEV, TOP)
    checked = jax.checkpoint(block_forward)

    def whole(params, stream):

        def one_sequence(sequence_item):
            return checked(params, sequence_item[0], sequence_item[1], sequence_item[2])
        result, hiddens = lax.map(one_sequence, (stream, doc_ids, routes))
        return (result, hiddens)
    result, pullback, hiddens = jax.vjp(whole, params, stream, has_aux=True)
    grad_params, grad_stream = pullback(cotangent.astype(jnp.float32).reshape(sequences, TOK_DEV, D))
    live_rows = (doc_ids > 0).astype(jnp.float32)[..., None]
    live_total = jnp.sum(live_rows) * D
    square_sums = jnp.stack([jnp.sum(live_rows * stream * stream), jnp.sum(live_rows * hiddens * hiddens), jnp.sum(live_rows * result * result)])
    residual_rms = jnp.sqrt(square_sums / live_total)
    output = result.reshape(-1, D).astype(jnp.bfloat16)
    input_grad = grad_stream.reshape(-1, D).astype(jnp.bfloat16)
    return (output, input_grad, grad_params[0], grad_params[1], grad_params[2], grad_params[3], grad_params[4], grad_params[5], grad_params[6], grad_params[7], grad_params[8], grad_params[9], grad_params[10], grad_params[11], residual_rms)
```

```python
import jax
import jax.numpy as jnp
from jax import lax
from jax.sharding import PartitionSpec as P

EPS = 1e-06
THETA = 10000.0
MASKED = -1e30
F32 = jnp.float32
BF16 = jnp.bfloat16


def rms_scale(field):
    return lax.rsqrt(jnp.mean(field * field, axis=-1, keepdims=True) + EPS)


def norm_back(field, scale, gain, upstream):
    weighted = upstream * gain
    inner = jnp.sum(weighted * field, axis=-1, keepdims=True)
    return scale * weighted - field * scale**3 * inner / field.shape[-1]


def rotary_tables(length, dim):
    half = dim // 2
    frequency = THETA ** (-2.0 * jnp.arange(half, dtype=F32) / dim)
    angles = jnp.arange(length, dtype=F32)[:, None] * frequency[None, :]
    return jnp.cos(angles), jnp.sin(angles)


def rotate(field, cosine, sine):
    half = field.shape[-1] // 2
    first, second = field[..., :half], field[..., half:]
    return jnp.concatenate(
        [first * cosine - second * sine, second * cosine + first * sine], axis=-1
    )


def dot(left, right):
    return jnp.dot(left, right, preferred_element_type=F32)


def dot_nt(left, right):
    return lax.dot_general(left, right, (((1,), (1,)), ((), ())), preferred_element_type=F32)


def dot_tn(left, right):
    return lax.dot_general(left, right, (((0,), (0,)), ((), ())), preferred_element_type=F32)


def gather(piece, axis, dim=0):
    return lax.all_gather(piece, axis, axis=dim, tiled=True)


def scatter_sum(whole, axis):
    return lax.psum_scatter(whole, axis, scatter_dimension=0, tiled=True)


def make_body(reps, shards):
    def body(
        tokens, cotangent, segment_ids, expert_ids, norm_gain, w_query, w_key, w_value, w_output,
        query_gain, key_gain, ffn_norm_gain, w_router, w_gate, w_up, w_down,
    ):
        length, width = tokens.shape
        head_size = query_gain.shape[0]
        head_count = width // head_size
        experts = w_gate.shape[0]
        hidden_total = w_gate.shape[2]
        heads = head_count // reps
        cols = heads * head_size
        parts = reps // experts
        sub = hidden_total // shards // parts
        hid = sub * shards
        rows = width // shards
        total = reps * length
        per_plane = reps // shards
        out_rows = cols // shards
        score_scale = head_size ** (-0.5)

        rep = lax.axis_index("rep")
        expert, part = rep // parts, rep % parts

        def columns(weight):
            return lax.dynamic_slice(weight, (0, rep * cols), (rows, cols))

        def hidden_columns(weight):
            own = lax.dynamic_slice(weight, (expert, 0, 0), (1, rows, hidden_total))
            own = own.reshape(rows, shards, parts, sub)
            return lax.dynamic_slice(own, (0, 0, part, 0), (rows, shards, 1, sub)).reshape(rows, hid)

        w_qkv = gather(jnp.concatenate([columns(w_query), columns(w_key), columns(w_value)], 1), "shard")
        there = [
            (src_rep * shards + src, (src * per_plane + src_rep % per_plane) * shards + src_rep // per_plane)
            for src_rep in range(reps)
            for src in range(shards)
        ]
        back = [(target, source) for source, target in there]
        first_row = (rep % per_plane) * cols + (rep // per_plane) * out_rows
        out_piece = lax.dynamic_slice(w_output, (first_row, 0), (out_rows, width))
        w_out = gather(lax.ppermute(out_piece, ("rep", "shard"), there), "shard")
        w_gu = gather(jnp.concatenate([hidden_columns(w_gate), hidden_columns(w_up)], 1), "shard")
        own_down = lax.dynamic_slice(w_down, (expert, part * sub, 0), (1, sub, width))
        w_dn = gather(own_down.reshape(sub, width), "shard")

        stream = tokens.astype(F32)
        live = (segment_ids > 0).astype(F32)[:, None]
        first_scale = rms_scale(stream)
        normed = (stream * first_scale * norm_gain).astype(BF16)
        grad_moe_own = jnp.where(segment_ids[:, None] > 0, cotangent, jnp.zeros_like(cotangent))

        normed_all = gather(normed, "rep")
        segments = gather(segment_ids, "rep").reshape(reps, length)
        routes = gather(expert_ids, "rep")
        grad_moe = gather(grad_moe_own, "rep")

        qkv = dot(normed_all, w_qkv)
        by_head = (reps, length, heads, head_size)
        query_raw = qkv[:, :cols].reshape(by_head)
        key_raw = qkv[:, cols : 2 * cols].reshape(by_head)
        value = qkv[:, 2 * cols :].astype(BF16).reshape(by_head)
        cosine, sine = rotary_tables(length, head_size)
        cosine, sine = cosine[:, None, :], sine[:, None, :]
        query_scale, key_scale = rms_scale(query_raw), rms_scale(key_raw)
        query = rotate(query_raw * query_scale * query_gain, cosine, sine).astype(BF16)
        key = rotate(key_raw * key_scale * key_gain, cosine, sine).astype(BF16)
        same = (segments[:, :, None] == segments[:, None, :])[:, None]
        scores = jnp.einsum("sqhd,skhd->shqk", query, key, preferred_element_type=F32) * score_scale
        scores = jnp.where(same, scores, MASKED)
        exponent = jnp.exp(scores - jnp.max(scores, axis=-1, keepdims=True))
        soft = exponent / jnp.sum(exponent, axis=-1, keepdims=True)
        soft_low = soft.astype(BF16)
        mixed = jnp.einsum("shqk,skhd->sqhd", soft_low, value, preferred_element_type=F32)
        mixed = mixed.astype(BF16).reshape(total, cols)
        attention_out = scatter_sum(dot(mixed, w_out).astype(BF16), "rep").astype(F32)

        hidden = stream + live * attention_out
        second_scale = rms_scale(hidden)
        normed_ffn = (hidden * second_scale * ffn_norm_gain).astype(BF16)
        ffn_all = gather(normed_ffn, "rep")

        def chances_of(field):
            logits = dot(field, w_router)
            shifted = jnp.exp(logits - jnp.max(logits, axis=-1, keepdims=True))
            return shifted / jnp.sum(shifted, axis=-1, keepdims=True)

        is_own = (jnp.arange(experts) == expert).astype(F32)
        chosen = jnp.any(routes == expert, axis=-1, keepdims=True).astype(F32)
        gate = jnp.sum(chances_of(ffn_all) * is_own, axis=-1, keepdims=True) * chosen
        gate_up = dot(ffn_all, w_gu)
        gate_pre, up_pre = gate_up[:, :hid], gate_up[:, hid:]
        sigmoid = jax.nn.sigmoid(gate_pre)
        silu = gate_pre * sigmoid
        inner = (silu * up_pre).astype(BF16)
        inner_gated = (gate * inner.astype(F32)).astype(BF16)
        grad_inner_raw = dot_nt(grad_moe, w_dn)
        grad_gate_part = jnp.sum(inner.astype(F32) * grad_inner_raw, axis=-1)
        grad_inner = gate * grad_inner_raw
        grad_gp = (grad_inner * up_pre * sigmoid * (1.0 + gate_pre * (1.0 - sigmoid))).astype(BF16)
        grad_up = (grad_inner * silu).astype(BF16)
        grad_gu = jnp.concatenate([grad_gp, grad_up], axis=1)
        moe_out = scatter_sum(dot(inner_gated, w_dn).astype(BF16), "rep").astype(F32)
        grad_ffn = scatter_sum(dot_nt(grad_gu, w_gu).astype(BF16), "rep").astype(F32)
        gate_parts = lax.all_gather(grad_gate_part.reshape(reps, length), "rep")
        gate_parts = lax.dynamic_index_in_dim(gate_parts, rep, 1, False)
        grad_chances = jnp.sum(gate_parts.reshape(experts, parts, length), axis=1).T
        picked = jnp.any(expert_ids[:, :, None] == jnp.arange(experts), axis=1)
        grad_chances = jnp.where(picked, grad_chances, 0.0)
        chances = chances_of(normed_ffn)
        grad_logits = chances * (
            grad_chances - jnp.sum(chances * grad_chances, axis=-1, keepdims=True)
        )
        grad_logits = grad_logits.astype(BF16)
        grad_router = dot_tn(normed_ffn, grad_logits)

        result = hidden + live * moe_out
        grad_result = cotangent.astype(F32)
        grad_normed_ffn = grad_ffn + dot_nt(grad_logits, w_router)
        grad_ffn_gain = jnp.sum(grad_normed_ffn * hidden * second_scale, axis=0)
        grad_hidden = grad_result + norm_back(hidden, second_scale, ffn_norm_gain, grad_normed_ffn)
        grad_attention = gather((live * grad_hidden).astype(BF16), "rep")

        grad_out_w = dot_tn(mixed, grad_attention)
        grad_mixed = dot_nt(grad_attention, w_out).astype(BF16).reshape(by_head)
        grad_value = jnp.einsum("shqk,sqhd->skhd", soft_low, grad_mixed, preferred_element_type=F32)
        grad_value = grad_value.astype(BF16)
        grad_probs = jnp.einsum("sqhd,skhd->shqk", grad_mixed, value, preferred_element_type=F32)
        row_dot = jnp.sum(soft * grad_probs, axis=-1, keepdims=True)
        grad_scores = (soft * (grad_probs - row_dot)).astype(BF16)
        grad_query = jnp.einsum("shqk,skhd->sqhd", grad_scores, key, preferred_element_type=F32)
        grad_key = jnp.einsum("shqk,sqhd->skhd", grad_scores, query, preferred_element_type=F32)
        grad_query = rotate(grad_query * score_scale, cosine, -sine)
        grad_key = rotate(grad_key * score_scale, cosine, -sine)
        grad_qgain = jnp.sum(grad_query * query_raw * query_scale, axis=(0, 1, 2))
        grad_kgain = jnp.sum(grad_key * key_raw * key_scale, axis=(0, 1, 2))
        grad_qkv = jnp.concatenate(
            [
                norm_back(query_raw, query_scale, query_gain, grad_query).reshape(total, cols).astype(BF16),
                norm_back(key_raw, key_scale, key_gain, grad_key).reshape(total, cols).astype(BF16),
                grad_value.reshape(total, cols),
            ],
            axis=1,
        )
        grad_normed = scatter_sum(dot_nt(grad_qkv, w_qkv).astype(BF16), "rep").astype(F32)
        grad_norm_gain = jnp.sum(grad_normed * stream * first_scale, axis=0)
        input_grad = grad_hidden + norm_back(stream, first_scale, norm_gain, grad_normed)

        sum_dn = scatter_sum(dot_tn(inner_gated, grad_moe).astype(BF16), "shard")
        sum_gu = scatter_sum(dot_tn(ffn_all, grad_gu).astype(BF16), "shard")
        sum_out = scatter_sum(grad_out_w.astype(BF16), "shard")
        sum_qkv = scatter_sum(dot_tn(normed_all, grad_qkv).astype(BF16), "shard")
        sum_out = lax.ppermute(sum_out, ("rep", "shard"), back)

        all_dn = gather(sum_dn, "rep").astype(F32).reshape(experts, parts * sub, width)
        all_gu = lax.all_gather(sum_gu, "rep").astype(F32)
        all_gu = all_gu.reshape(experts, parts, rows, 2, shards, sub).transpose(3, 0, 2, 4, 1, 5)
        all_gu = all_gu.reshape(2, experts, rows, hidden_total)
        all_out = gather(sum_out, "rep").astype(F32).reshape(shards, per_plane, out_rows, width)
        all_out = all_out.transpose(1, 0, 2, 3).reshape(rows, width)
        all_qkv = lax.all_gather(sum_qkv, "rep").astype(F32).reshape(reps, rows, 3, cols)
        all_qkv = all_qkv.transpose(2, 1, 0, 3).reshape(3, rows, width)

        square_sums = jnp.stack(
            [
                jnp.sum(live * stream * stream),
                jnp.sum(live * hidden * hidden),
                jnp.sum(live * result * result),
                jnp.sum(live),
            ]
        )
        norm_sum, qgain_sum, kgain_sum, ffn_sum, router_sum, stat_sum = lax.psum(
            (grad_norm_gain, grad_qgain, grad_kgain, grad_ffn_gain, grad_router, square_sums),
            ("rep", "shard"),
        )
        residual_rms = jnp.sqrt(stat_sum[:3] / (stat_sum[3] * width))
        return (
            result.astype(BF16), input_grad.astype(BF16), norm_sum,
            all_qkv[0], all_qkv[1], all_qkv[2], all_out,
            qgain_sum, kgain_sum, ffn_sum, router_sum,
            all_gu[0], all_gu[1], all_dn, residual_rms,
        )

    return body


def solution(mesh):
    by_token, by_shard, inner_shard = P(("rep", "shard"), None), P("shard", None), P(None, "shard", None)
    in_specs = (
        by_token, by_token, P(("rep", "shard")), by_token, P(),
        by_shard, by_shard, by_shard, by_shard, P(), P(), P(), P(),
        inner_shard, inner_shard, inner_shard,
    )
    out_specs = (
        by_token, by_token, P(), by_shard, by_shard, by_shard, by_shard, P(), P(), P(), P(),
        inner_shard, inner_shard, inner_shard, P(),
    )
    body = make_body(mesh.shape["rep"], mesh.shape["shard"])
    return jax.shard_map(body, mesh=mesh, in_specs=in_specs, out_specs=out_specs, check_vma=False)
```

```python
import functools

import jax
import jax.numpy as jnp
from jax import lax
from jax.experimental import pallas as pl
from jax.experimental.pallas import tpu as pltpu
from jax.sharding import PartitionSpec as P

EPS = 1e-06
THETA = 10000.0
MASKED = -1e30
F32 = jnp.float32
BF16 = jnp.bfloat16


def rms_scale(field):
    return lax.rsqrt(jnp.mean(field * field, axis=-1, keepdims=True) + EPS)


def norm_back(field, scale, gain, upstream):
    weighted = upstream * gain
    inner = jnp.sum(weighted * field, axis=-1, keepdims=True)
    return scale * weighted - field * scale**3 * inner / field.shape[-1]


def rotary_tables(length, dim):
    half = dim // 2
    frequency = THETA ** (-2.0 * jnp.arange(half, dtype=F32) / dim)
    angles = jnp.arange(length, dtype=F32)[:, None] * frequency[None, :]
    return jnp.cos(angles), jnp.sin(angles)


def rotate(field, cosine, sine):
    half = field.shape[-1] // 2
    first, second = field[..., :half], field[..., half:]
    return jnp.concatenate(
        [first * cosine - second * sine, second * cosine + first * sine], axis=-1
    )


def dot(left, right):
    return jnp.dot(left, right, preferred_element_type=F32)


def dot_nt(left, right):
    return lax.dot_general(left, right, (((1,), (1,)), ((), ())), preferred_element_type=F32)


def dot_tn(left, right):
    return lax.dot_general(left, right, (((0,), (0,)), ((), ())), preferred_element_type=F32)


def after(value, *events):
    return lax.optimization_barrier((value, *events))[0]


def total_over_all(value, sizes):
    for axis, size in sizes:
        bit = 1
        while bit < size:
            value = value + lax.ppermute(value, axis, [(i, i ^ bit) for i in range(size)])
            bit *= 2
    return value


def gather(piece, axis, dim=0):
    return lax.all_gather(piece, axis, axis=dim, tiled=True)


def scatter_sum(whole, axis):
    return lax.psum_scatter(whole, axis, scatter_dimension=0, tiled=True)


SCALE = 1.0
IDS = 16


def params(mib=24):
    return pltpu.CompilerParams(vmem_limit_bytes=mib * 2**20)


def whole(array):
    return pl.BlockSpec(array.shape, lambda i: (0,) * len(array.shape), pipeline_mode=pl.Buffered(1))


def cost(flops, arrays):
    moved = sum(a.size * a.dtype.itemsize for a in arrays)
    return pl.CostEstimate(flops=int(flops * SCALE), bytes_accessed=int(moved * SCALE), transcendentals=0)


def turned(rows):
    rows = jnp.concatenate([rows, jnp.zeros((128 - rows.shape[0], rows.shape[1]), F32)])
    return rows.T


def spin(field, cosine, sine):
    return field * cosine + pltpu.roll(field, field.shape[-1] // 2, 1) * sine


def head_state(raw, ids, gains, cosine, sine, cols, lane, score_scale):
    size = gains.shape[-1]
    query_raw = raw[:, lane : lane + size]
    key_raw = raw[:, cols + lane : cols + lane + size]
    value = raw[:, 2 * cols + lane : 2 * cols + lane + size].astype(BF16)
    query_scale, key_scale = rms_scale(query_raw), rms_scale(key_raw)
    query = spin(query_raw * query_scale * gains[0:1], cosine, sine).astype(BF16)
    key = spin(key_raw * key_scale * gains[1:2], cosine, sine).astype(BF16)
    scores = dot_nt(query, key) * score_scale
    scores = jnp.where(turned(ids)[:, 0:1] == ids[0:1], scores, MASKED)
    exponent = jnp.exp(scores - jnp.max(scores, axis=-1, keepdims=True))
    soft = exponent / jnp.sum(exponent, axis=-1, keepdims=True)
    return query_raw, key_raw, value, query_scale, key_scale, query, key, soft


def attend_kernel(length, score_scale, blk0, blk1, w_qkv, gains, cosine, sine, raw_ref, mixed_ref):
    size = gains.shape[-1]
    cols = w_qkv.shape[1] // 3
    raw = dot(jnp.concatenate([blk0[:length], blk1[:length]]), w_qkv[...])
    raw_ref[...] = raw
    for i, blk in enumerate((blk0, blk1)):
        ids = blk[length : length + IDS, :length].astype(F32)
        mine = raw[i * length : (i + 1) * length]
        for lane in range(0, cols, size):
            state = head_state(mine, ids, gains[...], cosine[...], sine[...], cols, lane, score_scale)
            value, soft = state[2], state[7]
            mixed = dot(soft.astype(BF16), value).astype(BF16)
            mixed_ref[i * length : (i + 1) * length, lane : lane + size] = mixed


def attend(pair, w_qkv, gains, cosine, sine, length, score_scale):
    width, cols = w_qkv.shape[0], w_qkv.shape[1] // 3
    ins = (*pair, w_qkv, gains, cosine, sine)
    specs = [whole(a) for a in ins]
    outs = (
        jax.ShapeDtypeStruct((2 * length, 3 * cols), F32),
        jax.ShapeDtypeStruct((2 * length, cols), BF16),
    )
    return pl.pallas_call(
        functools.partial(attend_kernel, length, score_scale),
        grid=(1,),
        in_specs=specs,
        out_specs=tuple(whole(a) for a in outs),
        out_shape=outs,
        compiler_params=params(),
        cost_estimate=cost(12 * length * width * cols, ins + outs),
        name="attend",
    )(*ins)


def attend_back_kernel(
    length, score_scale, da0, da1, blk0, blk1, raw_ref, w_qkv, w_out, gains, cosine, sine,
    out0, out1, grad_ref, gain_ref,
):
    cols = w_out.shape[0]
    size = gains.shape[-1]
    grad_mixed_all = dot_nt(jnp.concatenate([da0[...], da1[...]]), w_out[...]).astype(BF16)
    qgain = jnp.zeros((1, size), F32)
    kgain = jnp.zeros((1, size), F32)
    for i, (blk, out) in enumerate(((blk0, out0), (blk1, out1))):
        ids = blk[...].astype(F32)
        span = slice(i * length, (i + 1) * length)
        mine = raw_ref[span]
        for lane in range(0, cols, size):
            query_raw, key_raw, value, query_scale, key_scale, query, key, soft = head_state(
                mine, ids, gains[...], cosine[...], sine[...], cols, lane, score_scale
            )
            grad_mixed = grad_mixed_all[span, lane : lane + size]
            grad_value = dot_tn(soft.astype(BF16), grad_mixed).astype(BF16)
            grad_probs = dot_nt(grad_mixed, value)
            row_dot = jnp.sum(soft * grad_probs, axis=-1, keepdims=True)
            grad_scores = (soft * (grad_probs - row_dot)).astype(BF16)
            grad_query = spin(dot(grad_scores, key) * score_scale, cosine[...], -sine[...])
            grad_key = spin(dot_tn(grad_scores, query) * score_scale, cosine[...], -sine[...])
            qgain += jnp.sum(grad_query * query_raw * query_scale, axis=0, keepdims=True)
            kgain += jnp.sum(grad_key * key_raw * key_scale, axis=0, keepdims=True)
            grad_ref[span, lane : lane + size] = norm_back(
                query_raw, query_scale, gains[0:1], grad_query
            ).astype(BF16)
            grad_ref[span, cols + lane : cols + lane + size] = norm_back(
                key_raw, key_scale, gains[1:2], grad_key
            ).astype(BF16)
            grad_ref[span, 2 * cols + lane : 2 * cols + lane + size] = grad_value
        out[...] = dot_nt(grad_ref[span], w_qkv[...]).astype(BF16)
    gain_ref[...] = jnp.concatenate([qgain, kgain, jnp.zeros((6, size), F32)])


def attend_back(pair, ids, raw, w_qkv, w_out, gains, cosine, sine, length, score_scale):
    width, cols = w_qkv.shape[0], w_out.shape[0]
    ins = (*pair, *ids, raw, w_qkv, w_out, gains, cosine, sine)
    outs = (
        jax.ShapeDtypeStruct((length, width), BF16),
        jax.ShapeDtypeStruct((length, width), BF16),
        jax.ShapeDtypeStruct((2 * length, 3 * cols), BF16),
        jax.ShapeDtypeStruct((8, gains.shape[-1]), F32),
    )
    specs = [whole(a) for a in ins]
    for i in (2, 3):
        specs[i] = pl.BlockSpec((IDS, length), lambda i: (length // IDS, 0))
    return pl.pallas_call(
        functools.partial(attend_back_kernel, length, score_scale),
        grid=(1,),
        in_specs=specs,
        out_specs=tuple(whole(a) for a in outs),
        out_shape=outs,
        compiler_params=params(),
        cost_estimate=cost(24 * length * width * cols, ins + outs),
        name="attend_back",
    )(*ins)


def expert_in_kernel(
    length, experts, place, b0, b1, ids0, ids1, w_router, w_gu, gated_ref, inner_ref, factor_ref
):
    hid = w_gu.shape[1] // 2
    expert = place[1]
    field = joined((b0, b1))
    logits = dot(field, w_router[...])
    lane = lax.broadcasted_iota(jnp.int32, logits.shape, 1)
    logits = jnp.where(lane < experts, logits, MASKED)
    chances = jnp.exp(logits - jnp.max(logits, axis=-1, keepdims=True))
    chance = jnp.sum(jnp.where(lane == expert, chances, 0.0), axis=-1, keepdims=True)
    chance = chance / jnp.sum(chances, axis=-1, keepdims=True)
    routes = jnp.concatenate([turned(ids0[...].astype(F32)), turned(ids1[...].astype(F32))])
    wanted = expert.astype(F32)
    chosen = jnp.logical_or(routes[:, 1:2] == wanted, routes[:, 2:3] == wanted)
    gate = jnp.where(chosen, chance, 0.0)
    gate_up = dot(field, w_gu[...])
    gate_pre, up_pre = gate_up[:, :hid], gate_up[:, hid:]
    sigmoid = jax.nn.sigmoid(gate_pre)
    silu = gate_pre * sigmoid
    inner = (silu * up_pre).astype(BF16)
    inner_ref[...] = inner
    gated_ref[...] = (gate * inner.astype(F32)).astype(BF16)
    factor_ref[:, :hid] = gate * up_pre * sigmoid * (1.0 + gate_pre * (1.0 - sigmoid))
    factor_ref[:, hid:] = gate * silu


def expert_in(place, fields, ids, w_router, w_gu, length, experts):
    width, hid = fields[0].shape[1], w_gu.shape[1] // 2
    ins = (place, *fields, *ids, w_router, w_gu)
    outs = (
        jax.ShapeDtypeStruct((2 * length, hid), BF16),
        jax.ShapeDtypeStruct((2 * length, hid), BF16),
        jax.ShapeDtypeStruct((2 * length, 2 * hid), F32),
    )
    specs = [whole(a) for a in ins]
    specs[0] = pl.BlockSpec(memory_space=pltpu.SMEM)
    for i in (3, 4):
        specs[i] = pl.BlockSpec((IDS, length), lambda i: (length // IDS, 0))
    return pl.pallas_call(
        functools.partial(expert_in_kernel, length, experts),
        grid=(1,),
        in_specs=specs,
        out_specs=tuple(whole(a) for a in outs),
        out_shape=outs,
        compiler_params=params(28),
        cost_estimate=cost(8 * length * width * hid, ins + outs),
        name="expert_in",
    )(*ins)


def expert_back_kernel(length, place, c0, c1, inner, factor, w_gu, w_dn, out0, out1, grad_ref):
    hid = w_dn.shape[0]
    rep = place[0]
    grad_inner = dot_nt(joined((c0, c1)), w_dn[...])
    grad_gate = jnp.sum(inner[...].astype(F32) * grad_inner, axis=-1, keepdims=True)
    grad_ref[:, :hid] = (grad_inner * factor[:, :hid]).astype(BF16)
    grad_ref[:, hid:] = (grad_inner * factor[:, hid:]).astype(BF16)
    partial = dot_nt(grad_ref[...], w_gu[...]).astype(BF16)
    grad_gate = jnp.broadcast_to(grad_gate, (2 * length, 128)).T
    extra = out0.shape[0] - length
    row = lax.broadcasted_iota(jnp.int32, (extra, length), 0)
    for i, out in enumerate((out0, out1)):
        out[:length] = partial[i * length : (i + 1) * length]
        whole_grad = grad_gate[:extra, i * length : (i + 1) * length]
        high = whole_grad.astype(BF16).astype(F32)
        parts = jnp.where(row == 2 * rep, high, jnp.where(row == 2 * rep + 1, whole_grad - high, 0.0))
        out[length:, :length] = parts.astype(BF16)
        out[length:, length:] = jnp.zeros((extra, out.shape[1] - length), BF16)


def expert_back(place, grads, inner, factor, w_gu, w_dn, length, reps):
    width, hid = w_dn.shape[1], w_dn.shape[0]
    ins = (place, *grads, inner, factor, w_gu, w_dn)
    tall = length + max(2 * reps, IDS)
    outs = (
        jax.ShapeDtypeStruct((tall, width), BF16),
        jax.ShapeDtypeStruct((tall, width), BF16),
        jax.ShapeDtypeStruct((2 * length, 2 * hid), BF16),
    )
    specs = [whole(a) for a in ins]
    specs[0] = pl.BlockSpec(memory_space=pltpu.SMEM)
    return pl.pallas_call(
        functools.partial(expert_back_kernel, length),
        grid=(1,),
        in_specs=specs,
        out_specs=tuple(whole(a) for a in outs),
        out_shape=outs,
        compiler_params=params(30),
        cost_estimate=cost(12 * length * width * hid, ins + outs),
        name="expert_back",
    )(*ins)


def mix_out_kernel(length, mixed, w_out, out0, out1):
    both = dot(mixed[...], w_out[...]).astype(BF16)
    out0[...] = both[:length]
    out1[...] = both[length:]


def mix_out(mixed, w_out, length, name):
    out = jax.ShapeDtypeStruct((length, w_out.shape[1]), BF16)
    ins = (mixed, w_out)
    return pl.pallas_call(
        functools.partial(mix_out_kernel, length),
        grid=(1,),
        in_specs=[whole(a) for a in ins],
        out_specs=(whole(out), whole(out)),
        out_shape=(out, out),
        compiler_params=params(16),
        cost_estimate=cost(4 * length * w_out.size, (*ins, out, out)),
        name=name,
    )(*ins)


def joined(refs):
    return jnp.concatenate([ref[...] for ref in refs])


def weight_grad_kernel(count, *refs):
    refs[-1][...] = dot_tn(joined(refs[:count]), joined(refs[count:-1])).astype(BF16)


def weight_grad(left, right, tile, wide, name):
    out = jax.ShapeDtypeStruct((left[0].shape[1], right[0].shape[1]), BF16)
    ins = (*left, *right)
    rows_step, cols_step = int(tile < out.shape[0]), int(wide < out.shape[1])
    return pl.pallas_call(
        functools.partial(weight_grad_kernel, len(left)),
        grid=(out.shape[0] // tile if rows_step else out.shape[1] // wide,),
        in_specs=[pl.BlockSpec((a.shape[0], tile), lambda i: (0, i * rows_step)) for a in left]
        + [pl.BlockSpec((a.shape[0], wide), lambda i: (0, i * cols_step)) for a in right],
        out_specs=pl.BlockSpec((tile, wide), lambda i: (i * rows_step, i * cols_step)),
        out_shape=out,
        compiler_params=params(),
        cost_estimate=cost(2 * left[0].shape[0] * len(left) * out.size, (*ins, out)),
        name=name,
    )(*ins)


def attention_grad_kernel(count, out_rows, *refs):
    left, right, (extra, weight, out, gain) = refs[:count], refs[count:-4], refs[-4:]
    tile, columns = left[0].shape[1], right[0].shape[1]
    cols = out.shape[1] - columns
    grad = dot_tn(joined(left), joined(right))
    out[:, :columns] = grad.astype(BF16)
    gain[...] = jnp.sum(grad * weight[...].astype(F32), axis=-1, keepdims=True)
    chunks = extra.shape[1] // cols
    for k in range(tile // out_rows):
        place = pl.program_id(0) * (tile // out_rows) + k
        row = pl.multiple_of(lax.div(place, chunks) * out_rows, out_rows)
        lane = pl.multiple_of(lax.rem(place, chunks) * cols, cols)
        out[k * out_rows : (k + 1) * out_rows, columns:] = extra[pl.ds(row, out_rows), pl.ds(lane, cols)]


def attention_grad(left, right, extra, weight, length, shards, tile):
    width, columns, cols = left[0].shape[1], right[0].shape[1], extra.shape[0]
    outs = (jax.ShapeDtypeStruct((width, columns + cols), BF16), jax.ShapeDtypeStruct((width, 1), F32))
    return pl.pallas_call(
        functools.partial(attention_grad_kernel, len(left), cols // shards),
        grid=(width // tile,),
        in_specs=[pl.BlockSpec((length, tile), lambda i: (0, i)) for _ in left]
        + [pl.BlockSpec(a.shape, lambda i: (0, 0)) for a in (*right, extra)]
        + [pl.BlockSpec((tile, columns), lambda i: (i, 0))],
        out_specs=(
            pl.BlockSpec((tile, columns + cols), lambda i: (i, 0)),
            pl.BlockSpec((tile, 1), lambda i: (i, 0)),
        ),
        out_shape=outs,
        compiler_params=params(),
        cost_estimate=cost(2 * length * len(left) * width * columns, (*left, *right, *outs)),
        name="attention_grad",
    )(*left, *right, extra, weight)


def own_columns_kernel(place, query, key, value, out):
    cols = query.shape[1]
    for i, ref in enumerate((query, key, value)):
        out[:, i * cols : (i + 1) * cols] = ref[...]


def own_columns(weights, rep, cols):
    rows = weights[0].shape[0]
    return pl.pallas_call(
        own_columns_kernel,
        grid_spec=pltpu.PrefetchScalarGridSpec(
            num_scalar_prefetch=1,
            grid=(1,),
            in_specs=[pl.BlockSpec((rows, cols), lambda i, place: (0, place[0]))] * len(weights),
            out_specs=pl.BlockSpec((rows, len(weights) * cols), lambda i, place: (0, 0)),
        ),
        out_shape=jax.ShapeDtypeStruct((rows, len(weights) * cols), BF16),
        compiler_params=params(),
        name="own_columns",
    )(rep.reshape(1), *weights)


def own_expert_kernel(place, gate, up, down, gu, dn):
    step = pl.program_id(0)
    sub = gate.shape[2]
    for i, ref in enumerate((gate, up)):
        gu[:, pl.ds(pl.multiple_of(i * gu.shape[1] // 2 + step * sub, 128), sub)] = ref[0]

    @pl.when(step == 0)
    def _():
        dn[...] = down[0]


def own_expert(gate, up, down, table, parts, sub):
    _, rows, wide = gate.shape
    width = down.shape[2]
    hid = wide // parts
    spec = pl.BlockSpec((1, rows, sub), lambda z, place: (place[0], 0, z * parts + place[1]))
    return pl.pallas_call(
        own_expert_kernel,
        grid_spec=pltpu.PrefetchScalarGridSpec(
            num_scalar_prefetch=1,
            grid=(hid // sub,),
            in_specs=[spec, spec, pl.BlockSpec((1, sub, width), lambda z, place: (place[0], place[1], 0))],
            out_specs=(
                pl.BlockSpec((rows, 2 * hid), lambda z, place: (0, 0)),
                pl.BlockSpec((sub, width), lambda z, place: (0, 0)),
            ),
        ),
        out_shape=(jax.ShapeDtypeStruct((rows, 2 * hid), BF16), jax.ShapeDtypeStruct((sub, width), BF16)),
        compiler_params=params(),
        name="own_expert",
    )(table, gate, up, down)


def place_out_kernel(rows, place, *refs):
    out = refs[-1]
    cols = refs[0].shape[1]
    for m, source in enumerate(refs[:-1]):
        row = pl.multiple_of(place[m] * rows, rows)
        for c in range(out.shape[1] // cols):
            out[pl.ds(row, rows), c * cols : (c + 1) * cols] = source[c * rows : (c + 1) * rows].astype(F32)


def place_out(pieces, table, rows, shape):
    return pl.pallas_call(
        functools.partial(place_out_kernel, rows),
        grid_spec=pltpu.PrefetchScalarGridSpec(
            num_scalar_prefetch=1,
            grid=(1,),
            in_specs=[pl.BlockSpec((a.shape[0], a.shape[1] // 4), lambda i, place: (0, 3)) for a in pieces],
            out_specs=pl.BlockSpec(shape, lambda i, place: (0, 0)),
        ),
        out_shape=jax.ShapeDtypeStruct(shape, F32),
        compiler_params=params(),
        cost_estimate=cost(0, [jax.ShapeDtypeStruct((2, *shape), F32)]),
        name="place_out",
    )(table, *pieces)


def place_units_kernel(parts, shards, place, *refs):
    sources, (out_gate, out_up) = refs[:-2], refs[-2:]
    sub = sources[0].shape[1] // 2 // shards
    for m, source in enumerate(sources):
        expert, part = place[2 * m], place[2 * m + 1]
        for i, out in enumerate((out_gate, out_up)):
            for z in range(shards):
                lane = pl.multiple_of((z * parts + part) * sub, 128)
                at = (i * shards + z) * sub
                out[expert, :, pl.ds(lane, sub)] = source[:, at : at + sub].astype(F32)


def place_units(pieces, table, parts, shards, shape, tile):
    wide = pieces[0].shape[1]
    return pl.pallas_call(
        functools.partial(place_units_kernel, parts, shards),
        grid_spec=pltpu.PrefetchScalarGridSpec(
            num_scalar_prefetch=1,
            grid=(shape[1] // tile,),
            in_specs=[pl.BlockSpec((tile, wide), lambda t, place: (t, 0)) for _ in pieces],
            out_specs=[pl.BlockSpec((shape[0], tile, shape[2]), lambda t, place: (0, t, 0))] * 2,
        ),
        out_shape=[jax.ShapeDtypeStruct(shape, F32)] * 2,
        compiler_params=params(),
        cost_estimate=cost(0, [jax.ShapeDtypeStruct((4, *shape), F32)]),
        name="place_units",
    )(table, *pieces)


def place_down_kernel(place, *refs):
    sub = refs[0].shape[0]
    for m, source in enumerate(refs[:-1]):
        refs[-1][pl.ds(pl.multiple_of(place[m] * sub, sub), sub), :] = source[...].astype(F32)


def place_down(pieces, table, rows, sub, width):
    wide = pieces[0].shape[1]
    return pl.pallas_call(
        place_down_kernel,
        grid_spec=pltpu.PrefetchScalarGridSpec(
            num_scalar_prefetch=1,
            grid=(width // wide,),
            in_specs=[pl.BlockSpec((sub, wide), lambda c, place: (rows // sub + c, 0)) for _ in pieces],
            out_specs=pl.BlockSpec((len(pieces) * sub, wide), lambda c, place: (0, c)),
        ),
        out_shape=jax.ShapeDtypeStruct((len(pieces) * sub, width), F32),
        compiler_params=params(),
        cost_estimate=cost(0, [jax.ShapeDtypeStruct((len(pieces) * sub, 2 * width), F32)]),
        name="place_down",
    )(table, *pieces)


def place_heads_kernel(place, *refs):
    sources, outs = refs[:-3], refs[-3:]
    cols = sources[0].shape[1] // 4
    for m, source in enumerate(sources):
        lane = pl.multiple_of(place[m] * cols, cols)
        for i, out in enumerate(outs):
            out[:, pl.ds(lane, cols)] = source[:, i * cols : (i + 1) * cols].astype(F32)


def place_heads(pieces, table, tile):
    rows, wide = pieces[0].shape
    width = len(pieces) * wide // 4
    return pl.pallas_call(
        place_heads_kernel,
        grid_spec=pltpu.PrefetchScalarGridSpec(
            num_scalar_prefetch=1,
            grid=(rows // tile,),
            in_specs=[pl.BlockSpec((tile, wide), lambda t, place: (t, 0)) for _ in pieces],
            out_specs=[pl.BlockSpec((tile, width), lambda t, place: (t, 0))] * 3,
        ),
        out_shape=[jax.ShapeDtypeStruct((rows, width), F32)] * 3,
        compiler_params=params(),
        cost_estimate=cost(0, [jax.ShapeDtypeStruct((6, rows, width), F32)]),
        name="place_heads",
    )(table, *pieces)


def place_hidden_kernel(parts, shards, sub, source, *outs):
    hid = shards * sub
    for i, out in enumerate(outs):
        for z in range(shards):
            for p in range(parts):
                lane = i * hid + z * sub
                out[0, :, (z * parts + p) * sub : (z * parts + p + 1) * sub] = source[
                    p, :, lane : lane + sub
                ].astype(F32)


def place_hidden(source, experts, shards, tile):
    reps, rows, wide = source.shape
    parts = reps // experts
    full = parts * wide // 2
    return pl.pallas_call(
        functools.partial(place_hidden_kernel, parts, shards, wide // 2 // shards),
        grid=(experts, rows // tile),
        in_specs=[pl.BlockSpec((parts, tile, wide), lambda e, t: (e, t, 0))],
        out_specs=[pl.BlockSpec((1, tile, full), lambda e, t: (e, t, 0)) for _ in range(2)],
        out_shape=[jax.ShapeDtypeStruct((experts, rows, full), F32) for _ in range(2)],
        compiler_params=params(),
        name="place_hidden",
    )(source)


class Ring:
    def __init__(self, reps):
        self.reps = reps
        self.links = [m for m in range(2, reps, 2)]
        self.links.sort(key=lambda m: (bin(m).count("1"), m))

    def swap(self, piece, bit):
        return lax.ppermute(piece, "rep", [(i, i ^ bit) for i in range(self.reps)])

    @staticmethod
    def hops(m):
        return 1 << (m.bit_length() - 1), m & -m

    def gather(self, block):
        half = max(block.shape[0] // 32 * 16, 8)
        held = {0: block}
        for m in self.links:
            high, low = self.hops(m)
            if high == low:
                held[m] = self.swap(block, m)
            else:
                held[m] = jnp.concatenate(
                    [self.swap(held[m ^ high][:half], high), self.swap(held[m ^ low][half:], low)]
                )
        for m in [0] + self.links:
            held[m ^ 1] = self.swap(held[m], 1)
        return [held[m] for m in range(self.reps)]

    def summing(self):
        return RingSum(self)


class RingSum:
    def __init__(self, ring):
        self.ring = ring
        self.held = {}
        self.core = {}

    def feed(self, m, own, other):
        self.half = max(own.shape[0] // 32 * 16, 8)
        got = self.core[m] = self.ring.swap(other, 1)
        parts = (slice(None, self.half), slice(self.half, None))
        self.held[m] = [own[part].astype(F32) + got[part].astype(F32) for part in parts]

    def far(self, *gate):
        events = []
        for m in reversed(self.ring.links):
            high, low = self.ring.hops(m)
            if high == low:
                continue
            for part, bit in ((0, high), (1, low)):
                piece = self.held[m][part].astype(BF16)
                got = self.ring.swap(after(piece, *gate) if gate else piece, bit)
                self.held[m ^ bit][part] = self.held[m ^ bit][part] + got.astype(F32)
                events.append(got)
        return events

    def near(self, m, *gate):
        piece = jnp.concatenate(self.held[m]).astype(BF16)
        got = self.ring.swap(after(piece, *gate) if gate else piece, m)
        for part, rows in ((0, slice(None, self.half)), (1, slice(self.half, None))):
            self.held[0][part] = self.held[0][part] + got[rows].astype(F32)
        return got

    def total(self):
        return jnp.concatenate(self.held[0])


def make_body(reps, shards):
    ring = Ring(reps)

    def body(
        tokens, cotangent, segment_ids, expert_ids, norm_gain, w_query, w_key, w_value, w_output,
        query_gain, key_gain, ffn_norm_gain, w_router, w_gate, w_up, w_down,
    ):
        length, width = tokens.shape
        head_size = query_gain.shape[0]
        head_count = width // head_size
        experts = w_gate.shape[0]
        hidden_total = w_gate.shape[2]
        heads = head_count // reps
        cols = heads * head_size
        parts = reps // experts
        sub = hidden_total // shards // parts
        hid = sub * shards
        rows = width // shards
        total = reps * length
        per_plane = reps // shards
        out_rows = cols // shards
        score_scale = head_size ** (-0.5)

        rep = lax.axis_index("rep")
        expert, part = lax.div(rep, parts), lax.rem(rep, parts)

        def hidden_columns(weight):
            own = lax.dynamic_slice(weight, (expert, 0, 0), (1, rows, hidden_total))
            own = own.reshape(rows, shards, parts, sub)
            return lax.dynamic_slice(own, (0, 0, part, 0), (rows, shards, 1, sub)).reshape(rows, hid)

        there = [
            (src_rep * shards + src, (src * per_plane + src_rep % per_plane) * shards + src_rep // per_plane)
            for src_rep in range(reps)
            for src in range(shards)
        ]
        back = [(target, source) for source, target in there]
        first_row = lax.rem(rep, per_plane) * cols + lax.div(rep, per_plane) * out_rows
        out_piece = lax.dynamic_slice(w_output, (first_row, 0), (out_rows, width))
        out_piece = lax.ppermute(out_piece, ("rep", "shard"), there)
        w_qkv = gather(own_columns((w_query, w_key, w_value), rep, cols), "shard")

        stream = tokens.astype(F32)
        live = (segment_ids > 0).astype(F32)[:, None]
        first_scale = rms_scale(stream)
        normed = (stream * first_scale * norm_gain).astype(BF16)
        ids = jnp.concatenate([segment_ids[None], expert_ids.T]).astype(BF16)
        ids = jnp.pad(ids, ((0, IDS - ids.shape[0]), (0, width - length)))
        blocks = ring.gather(jnp.concatenate([normed, ids]))
        pairs = range(0, reps, 2)

        unit = jnp.stack([expert, part]).astype(jnp.int32)
        if sub % 128 == 0:
            own_gu, own_dn = own_expert(w_gate, w_up, w_down, unit, parts, sub)
        else:
            own_gu = jnp.concatenate([hidden_columns(w_gate), hidden_columns(w_up)], 1)
            own_dn = lax.dynamic_slice(w_down, (expert, part * sub, 0), (1, sub, width))[0]
        grad_moe_own = jnp.where(segment_ids[:, None] > 0, cotangent, jnp.zeros_like(cotangent))
        grad_moe = ring.gather(after(grad_moe_own, blocks[2], blocks[4]))
        arrived = [grad_moe[m] for m in ring.links]
        w_out = gather(after(out_piece, w_qkv, grad_moe[2], grad_moe[4]), "shard")
        w_gu = gather(after(own_gu, w_out), "shard")

        cosine, sine = rotary_tables(length, head_size)
        cosine = jnp.concatenate([cosine, cosine], axis=1)
        sine = jnp.concatenate([-sine, sine], axis=1)
        gains = after(jnp.stack([query_gain, key_gain]), own_gu, own_dn, *arrived)
        order = sorted(pairs, key=lambda m: (-bin(m).count("1"), m))
        singles = [m for m in ring.links if m & (m - 1) == 0]
        attended = {
            m: attend(blocks[m : m + 2], w_qkv, gains, cosine, sine, length, score_scale) for m in order
        }
        summed = ring.summing()
        for m in order:
            mixed = after(attended[m][1], attended[order[-1]][1]) if m != order[-1] else attended[m][1]
            summed.feed(m, *mix_out(mixed, w_out, length, "mix_out"))
        summed.far()
        near = [summed.near(m) for m in singles]
        attention_out = summed.total()
        w_dn = gather(after(own_dn, *near), "shard")

        hidden = stream + live * attention_out
        second_scale = rms_scale(hidden)
        normed_ffn = (hidden * second_scale * ffn_norm_gain).astype(BF16)
        ffn_all = ring.gather(normed_ffn)

        place = jnp.stack([rep, expert]).astype(jnp.int32)
        router = jnp.pad(w_router, ((0, 0), (0, 128 - experts)))
        entered = {m: expert_in(place, ffn_all[m : m + 2], blocks[m : m + 2], router, w_gu, length, experts) for m in order}
        inner_gated = [entered[m][0] for m in pairs]
        part_dn = weight_grad(inner_gated, grad_moe, hid, 512, "down_grad")
        sum_dn = scatter_sum(part_dn, "shard")
        stepped = {}
        summed = ring.summing()
        for i, m in enumerate(order):
            gate = [summed.core[order[i - 2]]] if i >= 2 else [part_dn]
            if i == len(order) - 1:
                gate += summed.far()
            stepped[m] = expert_back(
                after(place, *gate), grad_moe[m : m + 2], entered[m][1], entered[m][2], w_gu, w_dn, length, reps
            )
            summed.feed(m, *stepped[m][:2])
        near = [summed.near(m) for m in singles]
        grad_gu = [stepped[m][2] for m in pairs]
        grad_gu[0] = after(grad_gu[0], summed.core[order[-1]])
        part_gu = weight_grad(ffn_all, grad_gu, 256, 2 * hid, "up_grad")
        sum_gu = scatter_sum(after(part_gu, sum_dn, *near), "shard")
        grad_ffn = summed.total()
        grad_ffn = after(grad_ffn, part_gu)
        grad_gate = grad_ffn[length : length + 2 * reps, :length]
        grad_gate = jnp.sum(grad_gate.reshape(experts, parts * 2, length), axis=1)
        grad_ffn = grad_ffn[:length]

        logits = dot(normed_ffn, w_router)
        shifted = jnp.exp(logits - jnp.max(logits, axis=-1, keepdims=True))
        chances = shifted / jnp.sum(shifted, axis=-1, keepdims=True)
        picked = jnp.any(expert_ids[:, :, None] == jnp.arange(experts), axis=1)
        grad_chances = jnp.where(picked, grad_gate.T, 0.0)
        grad_logits = chances * (
            grad_chances - jnp.sum(chances * grad_chances, axis=-1, keepdims=True)
        )
        grad_logits = grad_logits.astype(BF16)
        grad_router = dot_tn(normed_ffn, grad_logits)

        grad_result = cotangent.astype(F32)
        grad_normed_ffn = grad_ffn + dot_nt(grad_logits, w_router)
        grad_ffn_gain = jnp.sum(grad_normed_ffn * hidden * second_scale, axis=0)
        grad_hidden = grad_result + norm_back(hidden, second_scale, ffn_norm_gain, grad_normed_ffn)
        grad_attention = ring.gather((live * grad_hidden).astype(BF16))

        moe_sum = ring.summing()
        for m in order:
            moe_sum.feed(m, *mix_out(after(entered[m][0], grad_attention[0]), w_dn, length, "mix_back"))
        backs = {}
        summed = ring.summing()
        backward = list(reversed(order))
        for i, m in enumerate(backward):
            gate = [moe_sum.core[order[min(i, len(order) - 1)]]]
            if i == len(order) - 1:
                gate += moe_sum.far()
            backs[m] = attend_back(
                grad_attention[m : m + 2], blocks[m : m + 2], attended[m][0],
                w_qkv, w_out, after(gains, *gate), cosine, sine, length, score_scale,
            )
            summed.feed(m, *backs[m][:2])
        mixed = [attended[m][1] for m in pairs]
        part_out = weight_grad(mixed, grad_attention, cols, 1024, "out_grad")
        grad_qkv = [backs[m][2] for m in pairs]
        grad_qkv[0] = after(grad_qkv[0], summed.core[backward[-1]])
        part_attention, grad_norm_gain = attention_grad(blocks, grad_qkv, part_out, w_qkv, length, shards, 256)
        grad_norm_gain = grad_norm_gain.reshape(-1) / norm_gain
        moe_last = [moe_sum.near(m) for m in singles]
        far = summed.far(*moe_last)
        normed_last = [summed.near(m) for m in singles]
        moe_out = moe_sum.total()
        grad_normed = summed.total()
        grad_gains = sum(backs[m][3] for m in pairs)
        grad_qgain, grad_kgain = grad_gains[0], grad_gains[1]
        input_grad = grad_hidden + norm_back(stream, first_scale, norm_gain, grad_normed)

        result = hidden + live * moe_out

        sum_attention = scatter_sum(after(part_attention, sum_gu, *moe_last), "shard")
        chops = [sum_dn[:, c : c + 2 * hid] for c in range(0, width, 2 * hid)]
        pieces = ring.gather(after(jnp.concatenate([sum_gu] + chops), *far))

        device = rep ^ jnp.arange(reps, dtype=jnp.int32)
        shapes = ((experts, rows, hidden_total),) * 2 + ((experts, parts * sub, width),)
        all_dn = place_down(pieces, device, rows, sub, width).reshape(shapes[2])
        if sub % 128 == 0:
            units = jnp.stack([lax.div(device, parts), lax.rem(device, parts)], axis=1).reshape(-1)
            all_gate, all_up = place_units(pieces, units, parts, shards, shapes[0], 64)
        else:
            all_gate, all_up = place_hidden(lax.all_gather(sum_gu, "rep"), experts, shards, rows // 4)
        sum_attention = after(sum_attention, *[pieces[m] for m in ring.links], *normed_last)
        sum_out = lax.ppermute(sum_attention[:, 3 * cols :], ("rep", "shard"), back)
        pieces = ring.gather(jnp.concatenate([sum_attention[:, : 3 * cols], sum_out], axis=1))
        all_qkv = place_heads(pieces, device, 64)
        row_block = lax.rem(device, per_plane) * shards + lax.div(device, per_plane)
        all_out = place_out(pieces, row_block, out_rows, (rows, width))

        square_sums = jnp.stack(
            [
                jnp.sum(live * stream * stream),
                jnp.sum(live * hidden * hidden),
                jnp.sum(live * result * result),
                jnp.sum(live),
            ]
        )
        small = [grad_norm_gain, grad_ffn_gain, grad_qgain, grad_kgain, grad_router.T.reshape(-1)]
        small.append(jnp.pad(square_sums, (0, 124)))
        small = total_over_all(
            jnp.concatenate([part.reshape(-1, 128) for part in small]), (("rep", reps), ("shard", shards))
        ).reshape(-1)
        norm_sum, ffn_sum = small[:width], small[width : 2 * width]
        small = small[2 * width :]
        qgain_sum, kgain_sum = small[:head_size], small[head_size : 2 * head_size]
        router_sum = small[2 * head_size : 2 * head_size + experts * width].reshape(experts, width).T
        stat_sum = small[2 * head_size + experts * width :]
        residual_rms = jnp.sqrt(stat_sum[:3] / (stat_sum[3] * width))
        return (
            result.astype(BF16), input_grad.astype(BF16), norm_sum,
            all_qkv[0], all_qkv[1], all_qkv[2], all_out,
            qgain_sum, kgain_sum, ffn_sum, router_sum,
            all_gate, all_up, all_dn, residual_rms,
        )

    return body


def solution(mesh):
    by_token, by_shard, inner_shard = P(("rep", "shard"), None), P("shard", None), P(None, "shard", None)
    in_specs = (
        by_token, by_token, P(("rep", "shard")), by_token, P(),
        by_shard, by_shard, by_shard, by_shard, P(), P(), P(), P(),
        inner_shard, inner_shard, inner_shard,
    )
    out_specs = (
        by_token, by_token, P(), by_shard, by_shard, by_shard, by_shard, P(), P(), P(), P(),
        inner_shard, inner_shard, inner_shard, P(),
    )
    body = make_body(mesh.shape["rep"], mesh.shape["shard"])
    return jax.shard_map(body, mesh=mesh, in_specs=in_specs, out_specs=out_specs, check_vma=False)
```

```python
import functools

import jax
import jax.numpy as jnp
from jax import lax
from jax.experimental import pallas as pl
from jax.experimental.pallas import tpu as pltpu
from jax.sharding import PartitionSpec as P

EPS = 1e-06
THETA = 10000.0
MASKED = -1e30
F32 = jnp.float32
BF16 = jnp.bfloat16


def rms_scale(field):
    return lax.rsqrt(jnp.mean(field * field, axis=-1, keepdims=True) + EPS)


def norm_back(field, scale, gain, upstream):
    weighted = upstream * gain
    inner = jnp.sum(weighted * field, axis=-1, keepdims=True)
    return scale * weighted - field * scale**3 * inner / field.shape[-1]


def rotary_tables(length, dim):
    half = dim // 2
    frequency = THETA ** (-2.0 * jnp.arange(half, dtype=F32) / dim)
    angles = jnp.arange(length, dtype=F32)[:, None] * frequency[None, :]
    return jnp.cos(angles), jnp.sin(angles)


def rotate(field, cosine, sine):
    half = field.shape[-1] // 2
    first, second = field[..., :half], field[..., half:]
    return jnp.concatenate(
        [first * cosine - second * sine, second * cosine + first * sine], axis=-1
    )


def dot(left, right):
    return jnp.dot(left, right, preferred_element_type=F32)


def dot_nt(left, right):
    return lax.dot_general(left, right, (((1,), (1,)), ((), ())), preferred_element_type=F32)


def dot_tn(left, right):
    return lax.dot_general(left, right, (((0,), (0,)), ((), ())), preferred_element_type=F32)


def after(value, *events):
    return lax.optimization_barrier((value, *events))[0]


def total_over_all(value, sizes):
    for axis, size in sizes:
        bit = 1
        while bit < size:
            value = value + lax.ppermute(value, axis, [(i, i ^ bit) for i in range(size)])
            bit *= 2
    return value


def gather(piece, axis, dim=0):
    return lax.all_gather(piece, axis, axis=dim, tiled=True)


def scatter_sum(whole, axis):
    return lax.psum_scatter(whole, axis, scatter_dimension=0, tiled=True)


IDS = 16


def params(mib=24):
    return pltpu.CompilerParams(vmem_limit_bytes=mib * 2**20)


def whole(array):
    return pl.BlockSpec(array.shape, lambda i: (0,) * len(array.shape), pipeline_mode=pl.Buffered(1))


def cost(flops, arrays):
    moved = sum(a.size * a.dtype.itemsize for a in arrays)
    return pl.CostEstimate(flops=flops, bytes_accessed=moved, transcendentals=0)


def turned(rows):
    rows = jnp.concatenate([rows, jnp.zeros((128 - rows.shape[0], rows.shape[1]), F32)])
    return rows.T


def spin(field, cosine, sine):
    return field * cosine + pltpu.roll(field, field.shape[-1] // 2, 1) * sine


def head_state(raw, ids, gains, cosine, sine, cols, lane, score_scale):
    size = gains.shape[-1]
    query_raw = raw[:, lane : lane + size]
    key_raw = raw[:, cols + lane : cols + lane + size]
    value = raw[:, 2 * cols + lane : 2 * cols + lane + size].astype(BF16)
    query_scale, key_scale = rms_scale(query_raw), rms_scale(key_raw)
    query = spin(query_raw * query_scale * gains[0:1], cosine, sine).astype(BF16)
    key = spin(key_raw * key_scale * gains[1:2], cosine, sine).astype(BF16)
    scores = dot_nt(query, key) * score_scale
    scores = jnp.where(turned(ids)[:, 0:1] == ids[0:1], scores, MASKED)
    exponent = jnp.exp(scores - jnp.max(scores, axis=-1, keepdims=True))
    soft = exponent / jnp.sum(exponent, axis=-1, keepdims=True)
    return query_raw, key_raw, value, query_scale, key_scale, query, key, soft


def attend_kernel(length, score_scale, blk0, blk1, w_qkv, gains, cosine, sine, raw_ref, mixed_ref):
    size = gains.shape[-1]
    cols = w_qkv.shape[1] // 3
    raw = dot(jnp.concatenate([blk0[:length], blk1[:length]]), w_qkv[...])
    raw_ref[...] = raw
    for i, blk in enumerate((blk0, blk1)):
        ids = blk[length : length + IDS, :length].astype(F32)
        mine = raw[i * length : (i + 1) * length]
        for lane in range(0, cols, size):
            state = head_state(mine, ids, gains[...], cosine[...], sine[...], cols, lane, score_scale)
            value, soft = state[2], state[7]
            mixed = dot(soft.astype(BF16), value).astype(BF16)
            mixed_ref[i * length : (i + 1) * length, lane : lane + size] = mixed


def attend(pair, w_qkv, gains, cosine, sine, length, score_scale):
    width, cols = w_qkv.shape[0], w_qkv.shape[1] // 3
    ins = (*pair, w_qkv, gains, cosine, sine)
    specs = [whole(a) for a in ins]
    outs = (
        jax.ShapeDtypeStruct((2 * length, 3 * cols), F32),
        jax.ShapeDtypeStruct((2 * length, cols), BF16),
    )
    return pl.pallas_call(
        functools.partial(attend_kernel, length, score_scale),
        grid=(1,),
        in_specs=specs,
        out_specs=tuple(whole(a) for a in outs),
        out_shape=outs,
        compiler_params=params(),
        cost_estimate=cost(12 * length * width * cols, ins + outs),
        name="attend",
    )(*ins)


def attend_back_kernel(
    length, score_scale, da0, da1, blk0, blk1, raw_ref, w_qkv, w_out, gains, cosine, sine,
    out0, out1, grad_ref, gain_ref,
):
    cols = w_out.shape[0]
    size = gains.shape[-1]
    grad_mixed_all = dot_nt(jnp.concatenate([da0[...], da1[...]]), w_out[...]).astype(BF16)
    qgain = jnp.zeros((1, size), F32)
    kgain = jnp.zeros((1, size), F32)
    for i, (blk, out) in enumerate(((blk0, out0), (blk1, out1))):
        ids = blk[...].astype(F32)
        span = slice(i * length, (i + 1) * length)
        mine = raw_ref[span]
        for lane in range(0, cols, size):
            query_raw, key_raw, value, query_scale, key_scale, query, key, soft = head_state(
                mine, ids, gains[...], cosine[...], sine[...], cols, lane, score_scale
            )
            grad_mixed = grad_mixed_all[span, lane : lane + size]
            grad_value = dot_tn(soft.astype(BF16), grad_mixed).astype(BF16)
            grad_probs = dot_nt(grad_mixed, value)
            row_dot = jnp.sum(soft * grad_probs, axis=-1, keepdims=True)
            grad_scores = (soft * (grad_probs - row_dot)).astype(BF16)
            grad_query = spin(dot(grad_scores, key) * score_scale, cosine[...], -sine[...])
            grad_key = spin(dot_tn(grad_scores, query) * score_scale, cosine[...], -sine[...])
            qgain += jnp.sum(grad_query * query_raw * query_scale, axis=0, keepdims=True)
            kgain += jnp.sum(grad_key * key_raw * key_scale, axis=0, keepdims=True)
            grad_ref[span, lane : lane + size] = norm_back(
                query_raw, query_scale, gains[0:1], grad_query
            ).astype(BF16)
            grad_ref[span, cols + lane : cols + lane + size] = norm_back(
                key_raw, key_scale, gains[1:2], grad_key
            ).astype(BF16)
            grad_ref[span, 2 * cols + lane : 2 * cols + lane + size] = grad_value
        out[...] = dot_nt(grad_ref[span], w_qkv[...]).astype(BF16)
    gain_ref[...] = jnp.concatenate([qgain, kgain, jnp.zeros((6, size), F32)])


def attend_back(pair, ids, raw, w_qkv, w_out, gains, cosine, sine, length, score_scale):
    width, cols = w_qkv.shape[0], w_out.shape[0]
    ins = (*pair, *ids, raw, w_qkv, w_out, gains, cosine, sine)
    outs = (
        jax.ShapeDtypeStruct((length, width), BF16),
        jax.ShapeDtypeStruct((length, width), BF16),
        jax.ShapeDtypeStruct((2 * length, 3 * cols), BF16),
        jax.ShapeDtypeStruct((8, gains.shape[-1]), F32),
    )
    specs = [whole(a) for a in ins]
    for i in (2, 3):
        specs[i] = pl.BlockSpec((IDS, length), lambda i: (length // IDS, 0))
    return pl.pallas_call(
        functools.partial(attend_back_kernel, length, score_scale),
        grid=(1,),
        in_specs=specs,
        out_specs=tuple(whole(a) for a in outs),
        out_shape=outs,
        compiler_params=params(),
        cost_estimate=cost(24 * length * width * cols, ins + outs),
        name="attend_back",
    )(*ins)


def expert_in_kernel(
    length, experts, place, b0, b1, ids0, ids1, w_router, w_gu, gated_ref, inner_ref, factor_ref
):
    hid = w_gu.shape[1] // 2
    expert = place[1]
    field = joined((b0, b1))
    logits = dot(field, w_router[...])
    lane = lax.broadcasted_iota(jnp.int32, logits.shape, 1)
    logits = jnp.where(lane < experts, logits, MASKED)
    chances = jnp.exp(logits - jnp.max(logits, axis=-1, keepdims=True))
    chance = jnp.sum(jnp.where(lane == expert, chances, 0.0), axis=-1, keepdims=True)
    chance = chance / jnp.sum(chances, axis=-1, keepdims=True)
    routes = jnp.concatenate([turned(ids0[...].astype(F32)), turned(ids1[...].astype(F32))])
    wanted = expert.astype(F32)
    chosen = jnp.logical_or(routes[:, 1:2] == wanted, routes[:, 2:3] == wanted)
    gate = jnp.where(chosen, chance, 0.0)
    gate_up = dot(field, w_gu[...])
    gate_pre, up_pre = gate_up[:, :hid], gate_up[:, hid:]
    sigmoid = jax.nn.sigmoid(gate_pre)
    silu = gate_pre * sigmoid
    inner = (silu * up_pre).astype(BF16)
    inner_ref[...] = inner
    gated_ref[...] = (gate * inner.astype(F32)).astype(BF16)
    factor_ref[:, :hid] = gate * up_pre * sigmoid * (1.0 + gate_pre * (1.0 - sigmoid))
    factor_ref[:, hid:] = gate * silu


def expert_in(place, fields, ids, w_router, w_gu, length, experts):
    width, hid = fields[0].shape[1], w_gu.shape[1] // 2
    ins = (place, *fields, *ids, w_router, w_gu)
    outs = (
        jax.ShapeDtypeStruct((2 * length, hid), BF16),
        jax.ShapeDtypeStruct((2 * length, hid), BF16),
        jax.ShapeDtypeStruct((2 * length, 2 * hid), F32),
    )
    specs = [whole(a) for a in ins]
    specs[0] = pl.BlockSpec(memory_space=pltpu.SMEM)
    for i in (3, 4):
        specs[i] = pl.BlockSpec((IDS, length), lambda i: (length // IDS, 0))
    return pl.pallas_call(
        functools.partial(expert_in_kernel, length, experts),
        grid=(1,),
        in_specs=specs,
        out_specs=tuple(whole(a) for a in outs),
        out_shape=outs,
        compiler_params=params(28),
        cost_estimate=cost(8 * length * width * hid, ins + outs),
        name="expert_in",
    )(*ins)


def expert_back_kernel(length, place, c0, c1, inner, factor, w_gu, w_dn, out0, out1, grad_ref):
    hid = w_dn.shape[0]
    rep = place[0]
    grad_inner = dot_nt(joined((c0, c1)), w_dn[...])
    grad_gate = jnp.sum(inner[...].astype(F32) * grad_inner, axis=-1, keepdims=True)
    grad_ref[:, :hid] = (grad_inner * factor[:, :hid]).astype(BF16)
    grad_ref[:, hid:] = (grad_inner * factor[:, hid:]).astype(BF16)
    partial = dot_nt(grad_ref[...], w_gu[...]).astype(BF16)
    grad_gate = jnp.broadcast_to(grad_gate, (2 * length, 128)).T
    extra = out0.shape[0] - length
    row = lax.broadcasted_iota(jnp.int32, (extra, length), 0)
    for i, out in enumerate((out0, out1)):
        out[:length] = partial[i * length : (i + 1) * length]
        whole_grad = grad_gate[:extra, i * length : (i + 1) * length]
        high = whole_grad.astype(BF16).astype(F32)
        parts = jnp.where(row == 2 * rep, high, jnp.where(row == 2 * rep + 1, whole_grad - high, 0.0))
        out[length:, :length] = parts.astype(BF16)
        out[length:, length:] = jnp.zeros((extra, out.shape[1] - length), BF16)


def expert_back(place, grads, inner, factor, w_gu, w_dn, length, reps):
    width, hid = w_dn.shape[1], w_dn.shape[0]
    ins = (place, *grads, inner, factor, w_gu, w_dn)
    tall = length + max(2 * reps, IDS)
    outs = (
        jax.ShapeDtypeStruct((tall, width), BF16),
        jax.ShapeDtypeStruct((tall, width), BF16),
        jax.ShapeDtypeStruct((2 * length, 2 * hid), BF16),
    )
    specs = [whole(a) for a in ins]
    specs[0] = pl.BlockSpec(memory_space=pltpu.SMEM)
    return pl.pallas_call(
        functools.partial(expert_back_kernel, length),
        grid=(1,),
        in_specs=specs,
        out_specs=tuple(whole(a) for a in outs),
        out_shape=outs,
        compiler_params=params(30),
        cost_estimate=cost(12 * length * width * hid, ins + outs),
        name="expert_back",
    )(*ins)


def mix_out_kernel(length, mixed, w_out, out0, out1):
    both = dot(mixed[...], w_out[...]).astype(BF16)
    out0[...] = both[:length]
    out1[...] = both[length:]


def mix_out(mixed, w_out, length, name):
    out = jax.ShapeDtypeStruct((length, w_out.shape[1]), BF16)
    ins = (mixed, w_out)
    return pl.pallas_call(
        functools.partial(mix_out_kernel, length),
        grid=(1,),
        in_specs=[whole(a) for a in ins],
        out_specs=(whole(out), whole(out)),
        out_shape=(out, out),
        compiler_params=params(16),
        cost_estimate=cost(4 * length * w_out.size, (*ins, out, out)),
        name=name,
    )(*ins)


def joined(refs):
    return jnp.concatenate([ref[...] for ref in refs])


def weight_grad_kernel(count, *refs):
    refs[-1][...] = dot_tn(joined(refs[:count]), joined(refs[count:-1])).astype(BF16)


def weight_grad(left, right, tile, wide, name):
    out = jax.ShapeDtypeStruct((left[0].shape[1], right[0].shape[1]), BF16)
    ins = (*left, *right)
    rows_step, cols_step = int(tile < out.shape[0]), int(wide < out.shape[1])
    return pl.pallas_call(
        functools.partial(weight_grad_kernel, len(left)),
        grid=(out.shape[0] // tile if rows_step else out.shape[1] // wide,),
        in_specs=[pl.BlockSpec((a.shape[0], tile), lambda i: (0, i * rows_step)) for a in left]
        + [pl.BlockSpec((a.shape[0], wide), lambda i: (0, i * cols_step)) for a in right],
        out_specs=pl.BlockSpec((tile, wide), lambda i: (i * rows_step, i * cols_step)),
        out_shape=out,
        compiler_params=params(),
        cost_estimate=cost(2 * left[0].shape[0] * len(left) * out.size, (*ins, out)),
        name=name,
    )(*ins)


def attention_grad_kernel(count, out_rows, *refs):
    left, right, (extra, weight, out, gain) = refs[:count], refs[count:-4], refs[-4:]
    tile, columns = left[0].shape[1], right[0].shape[1]
    cols = out.shape[1] - columns
    grad = dot_tn(joined(left), joined(right))
    out[:, :columns] = grad.astype(BF16)
    gain[...] = jnp.sum(grad * weight[...].astype(F32), axis=-1, keepdims=True)
    chunks = extra.shape[1] // cols
    for k in range(tile // out_rows):
        place = pl.program_id(0) * (tile // out_rows) + k
        row = pl.multiple_of(lax.div(place, chunks) * out_rows, out_rows)
        lane = pl.multiple_of(lax.rem(place, chunks) * cols, cols)
        out[k * out_rows : (k + 1) * out_rows, columns:] = extra[pl.ds(row, out_rows), pl.ds(lane, cols)]


def attention_grad(left, right, extra, weight, length, shards, tile):
    width, columns, cols = left[0].shape[1], right[0].shape[1], extra.shape[0]
    outs = (jax.ShapeDtypeStruct((width, columns + cols), BF16), jax.ShapeDtypeStruct((width, 1), F32))
    return pl.pallas_call(
        functools.partial(attention_grad_kernel, len(left), cols // shards),
        grid=(width // tile,),
        in_specs=[pl.BlockSpec((length, tile), lambda i: (0, i)) for _ in left]
        + [pl.BlockSpec(a.shape, lambda i: (0, 0)) for a in (*right, extra)]
        + [pl.BlockSpec((tile, columns), lambda i: (i, 0))],
        out_specs=(
            pl.BlockSpec((tile, columns + cols), lambda i: (i, 0)),
            pl.BlockSpec((tile, 1), lambda i: (i, 0)),
        ),
        out_shape=outs,
        compiler_params=params(),
        cost_estimate=cost(2 * length * len(left) * width * columns, (*left, *right, *outs)),
        name="attention_grad",
    )(*left, *right, extra, weight)


def own_columns_kernel(place, query, key, value, out):
    cols = query.shape[1]
    for i, ref in enumerate((query, key, value)):
        out[:, i * cols : (i + 1) * cols] = ref[...]


def own_columns(weights, rep, cols):
    rows = weights[0].shape[0]
    return pl.pallas_call(
        own_columns_kernel,
        grid_spec=pltpu.PrefetchScalarGridSpec(
            num_scalar_prefetch=1,
            grid=(1,),
            in_specs=[pl.BlockSpec((rows, cols), lambda i, place: (0, place[0]))] * len(weights),
            out_specs=pl.BlockSpec((rows, len(weights) * cols), lambda i, place: (0, 0)),
        ),
        out_shape=jax.ShapeDtypeStruct((rows, len(weights) * cols), BF16),
        compiler_params=params(),
        name="own_columns",
    )(rep.reshape(1), *weights)


def own_expert_kernel(place, gate, up, down, gu, dn):
    step = pl.program_id(0)
    sub = gate.shape[2]
    for i, ref in enumerate((gate, up)):
        gu[:, pl.ds(pl.multiple_of(i * gu.shape[1] // 2 + step * sub, 128), sub)] = ref[0]

    @pl.when(step == 0)
    def _():
        dn[...] = down[0]


def own_expert(gate, up, down, table, parts, sub):
    _, rows, wide = gate.shape
    width = down.shape[2]
    hid = wide // parts
    spec = pl.BlockSpec((1, rows, sub), lambda z, place: (place[0], 0, z * parts + place[1]))
    return pl.pallas_call(
        own_expert_kernel,
        grid_spec=pltpu.PrefetchScalarGridSpec(
            num_scalar_prefetch=1,
            grid=(hid // sub,),
            in_specs=[spec, spec, pl.BlockSpec((1, sub, width), lambda z, place: (place[0], place[1], 0))],
            out_specs=(
                pl.BlockSpec((rows, 2 * hid), lambda z, place: (0, 0)),
                pl.BlockSpec((sub, width), lambda z, place: (0, 0)),
            ),
        ),
        out_shape=(jax.ShapeDtypeStruct((rows, 2 * hid), BF16), jax.ShapeDtypeStruct((sub, width), BF16)),
        compiler_params=params(),
        name="own_expert",
    )(table, gate, up, down)


def place_out_kernel(rows, place, *refs):
    out = refs[-1]
    cols = refs[0].shape[1]
    for m, source in enumerate(refs[:-1]):
        row = pl.multiple_of(place[m] * rows, rows)
        for c in range(out.shape[1] // cols):
            out[pl.ds(row, rows), c * cols : (c + 1) * cols] = source[c * rows : (c + 1) * rows].astype(F32)


def place_out(pieces, table, rows, shape):
    return pl.pallas_call(
        functools.partial(place_out_kernel, rows),
        grid_spec=pltpu.PrefetchScalarGridSpec(
            num_scalar_prefetch=1,
            grid=(1,),
            in_specs=[pl.BlockSpec(a.shape, lambda i, place: (0, 0)) for a in pieces],
            out_specs=pl.BlockSpec(shape, lambda i, place: (0, 0)),
        ),
        out_shape=jax.ShapeDtypeStruct(shape, F32),
        compiler_params=params(),
        cost_estimate=cost(0, [jax.ShapeDtypeStruct((2, *shape), F32)]),
        name="place_out",
    )(table, *pieces)


def place_units_kernel(parts, shards, place, *refs):
    sources, (out_gate, out_up) = refs[:-2], refs[-2:]
    sub = sources[0].shape[1] // 2 // shards
    for m, source in enumerate(sources):
        expert, part = place[2 * m], place[2 * m + 1]
        for i, out in enumerate((out_gate, out_up)):
            for z in range(shards):
                lane = pl.multiple_of((z * parts + part) * sub, 128)
                at = (i * shards + z) * sub
                out[expert, :, pl.ds(lane, sub)] = source[:, at : at + sub].astype(F32)


def place_units(pieces, table, parts, shards, shape, tile):
    wide = pieces[0].shape[1]
    return pl.pallas_call(
        functools.partial(place_units_kernel, parts, shards),
        grid_spec=pltpu.PrefetchScalarGridSpec(
            num_scalar_prefetch=1,
            grid=(shape[1] // tile,),
            in_specs=[pl.BlockSpec((tile, wide), lambda t, place: (t, 0)) for _ in pieces],
            out_specs=[pl.BlockSpec((shape[0], tile, shape[2]), lambda t, place: (0, t, 0))] * 2,
        ),
        out_shape=[jax.ShapeDtypeStruct(shape, F32)] * 2,
        compiler_params=params(),
        cost_estimate=cost(0, [jax.ShapeDtypeStruct((4, *shape), F32)]),
        name="place_units",
    )(table, *pieces)


def place_down_kernel(place, *refs):
    sub = refs[0].shape[0]
    for m, source in enumerate(refs[:-1]):
        refs[-1][pl.ds(pl.multiple_of(place[m] * sub, sub), sub), :] = source[...].astype(F32)


def place_down(pieces, table, rows, sub, width):
    wide = pieces[0].shape[1]
    return pl.pallas_call(
        place_down_kernel,
        grid_spec=pltpu.PrefetchScalarGridSpec(
            num_scalar_prefetch=1,
            grid=(width // wide,),
            in_specs=[pl.BlockSpec((sub, wide), lambda c, place: (rows // sub + c, 0)) for _ in pieces],
            out_specs=pl.BlockSpec((len(pieces) * sub, wide), lambda c, place: (0, c)),
        ),
        out_shape=jax.ShapeDtypeStruct((len(pieces) * sub, width), F32),
        compiler_params=params(),
        cost_estimate=cost(0, [jax.ShapeDtypeStruct((len(pieces) * sub, 2 * width), F32)]),
        name="place_down",
    )(table, *pieces)


def place_columns_kernel(source, *outs):
    cols = outs[0].shape[1]
    for i, out in enumerate(outs):
        out[...] = source[0, :, i * cols : (i + 1) * cols].astype(F32)


def place_columns(source, rows, count):
    reps, _, wide = source.shape
    cols = wide // count
    return pl.pallas_call(
        place_columns_kernel,
        grid=(reps,),
        in_specs=[pl.BlockSpec((1, rows, wide), lambda r: (r, 0, 0))],
        out_specs=[pl.BlockSpec((rows, cols), lambda r: (0, r)) for _ in range(count)],
        out_shape=[jax.ShapeDtypeStruct((rows, reps * cols), F32) for _ in range(count)],
        compiler_params=params(),
        name="place_columns",
    )(source)


def place_hidden_kernel(parts, shards, sub, source, *outs):
    hid = shards * sub
    for i, out in enumerate(outs):
        for z in range(shards):
            for p in range(parts):
                lane = i * hid + z * sub
                out[0, :, (z * parts + p) * sub : (z * parts + p + 1) * sub] = source[
                    p, :, lane : lane + sub
                ].astype(F32)


def place_hidden(source, experts, shards, tile):
    reps, rows, wide = source.shape
    parts = reps // experts
    full = parts * wide // 2
    return pl.pallas_call(
        functools.partial(place_hidden_kernel, parts, shards, wide // 2 // shards),
        grid=(experts, rows // tile),
        in_specs=[pl.BlockSpec((parts, tile, wide), lambda e, t: (e, t, 0))],
        out_specs=[pl.BlockSpec((1, tile, full), lambda e, t: (e, t, 0)) for _ in range(2)],
        out_shape=[jax.ShapeDtypeStruct((experts, rows, full), F32) for _ in range(2)],
        compiler_params=params(),
        name="place_hidden",
    )(source)


class Ring:
    def __init__(self, reps):
        self.reps = reps
        self.links = [m for m in range(2, reps, 2)]
        self.links.sort(key=lambda m: (bin(m).count("1"), m))
        self.singles = [m for m in self.links if m & (m - 1) == 0]

    def swap(self, piece, bit):
        return lax.ppermute(piece, "rep", [(i, i ^ bit) for i in range(self.reps)])

    @staticmethod
    def hops(m):
        return 1 << (m.bit_length() - 1), m & -m

    def gathering(self, block):
        return RingGather(self, block)

    def gather(self, block):
        whole_set = RingGather(self, block)
        whole_set.near()
        whole_set.far()
        for m in [0] + self.links:
            whole_set.core(m)
        return whole_set.blocks()

    def summing(self):
        return RingSum(self)


class RingGather:
    def __init__(self, ring, block):
        self.ring = ring
        self.half = max(block.shape[0] // 32 * 16, 8)
        self.held = {0: block}

    def near(self, *gate):
        block = after(self.held[0], *gate) if gate else self.held[0]
        for m in self.ring.singles:
            self.held[m] = self.ring.swap(block, m)

    def far(self, *gate):
        for m in self.ring.links:
            high, low = self.ring.hops(m)
            if high == low:
                continue
            first, second = self.held[m ^ high][: self.half], self.held[m ^ low][self.half :]
            if gate:
                first, second = after((first, second), *gate)
            self.held[m] = jnp.concatenate([self.ring.swap(first, high), self.ring.swap(second, low)])

    def core(self, m, *gate):
        block = after(self.held[m], *gate) if gate else self.held[m]
        self.held[m ^ 1] = self.ring.swap(block, 1)

    def pair(self, m):
        return [self.held[m], self.held[m ^ 1]]

    def blocks(self):
        return [self.held[m] for m in range(self.ring.reps)]


class RingSum:
    def __init__(self, ring):
        self.ring = ring
        self.held = {}
        self.core = {}

    def feed(self, m, own, other):
        self.half = max(own.shape[0] // 32 * 16, 8)
        got = self.core[m] = self.ring.swap(other, 1)
        parts = (slice(None, self.half), slice(self.half, None))
        self.held[m] = [own[part].astype(F32) + got[part].astype(F32) for part in parts]

    def far(self, *gate):
        events = []
        for m in reversed(self.ring.links):
            high, low = self.ring.hops(m)
            if high == low:
                continue
            for part, bit in ((0, high), (1, low)):
                piece = self.held[m][part].astype(BF16)
                got = self.ring.swap(after(piece, *gate) if gate else piece, bit)
                self.held[m ^ bit][part] = self.held[m ^ bit][part] + got.astype(F32)
                events.append(got)
        return events

    def near(self, m, *gate):
        piece = jnp.concatenate(self.held[m]).astype(BF16)
        got = self.ring.swap(after(piece, *gate) if gate else piece, m)
        for part, rows in ((0, slice(None, self.half)), (1, slice(self.half, None))):
            self.held[0][part] = self.held[0][part] + got[rows].astype(F32)
        return got

    def total(self):
        return jnp.concatenate(self.held[0])


def make_body(reps, shards):
    ring = Ring(reps)

    def body(
        tokens, cotangent, segment_ids, expert_ids, norm_gain, w_query, w_key, w_value, w_output,
        query_gain, key_gain, ffn_norm_gain, w_router, w_gate, w_up, w_down,
    ):
        length, width = tokens.shape
        head_size = query_gain.shape[0]
        head_count = width // head_size
        experts = w_gate.shape[0]
        hidden_total = w_gate.shape[2]
        heads = head_count // reps
        cols = heads * head_size
        parts = reps // experts
        sub = hidden_total // shards // parts
        hid = sub * shards
        rows = width // shards
        total = reps * length
        per_plane = reps // shards
        out_rows = cols // shards
        score_scale = head_size ** (-0.5)

        rep = lax.axis_index("rep")
        expert, part = lax.div(rep, parts), lax.rem(rep, parts)

        def hidden_columns(weight):
            own = lax.dynamic_slice(weight, (expert, 0, 0), (1, rows, hidden_total))
            own = own.reshape(rows, shards, parts, sub)
            return lax.dynamic_slice(own, (0, 0, part, 0), (rows, shards, 1, sub)).reshape(rows, hid)

        there = [
            (src_rep * shards + src, (src * per_plane + src_rep % per_plane) * shards + src_rep // per_plane)
            for src_rep in range(reps)
            for src in range(shards)
        ]
        back = [(target, source) for source, target in there]
        first_row = lax.rem(rep, per_plane) * cols + lax.div(rep, per_plane) * out_rows
        out_piece = lax.dynamic_slice(w_output, (first_row, 0), (out_rows, width))
        out_piece = lax.ppermute(out_piece, ("rep", "shard"), there)
        w_qkv = gather(own_columns((w_query, w_key, w_value), rep, cols), "shard")

        stream = tokens.astype(F32)
        live = (segment_ids > 0).astype(F32)[:, None]
        first_scale = rms_scale(stream)
        normed = (stream * first_scale * norm_gain).astype(BF16)
        ids = jnp.concatenate([segment_ids[None], expert_ids.T]).astype(BF16)
        ids = jnp.pad(ids, ((0, IDS - ids.shape[0]), (0, width - length)))
        first = ring.gathering(jnp.concatenate([normed, ids]))
        first.near()
        pairs = range(0, reps, 2)

        unit = jnp.stack([expert, part]).astype(jnp.int32)
        if sub % 128 == 0:
            own_gu, own_dn = own_expert(w_gate, w_up, w_down, unit, parts, sub)
        else:
            own_gu = jnp.concatenate([hidden_columns(w_gate), hidden_columns(w_up)], 1)
            own_dn = lax.dynamic_slice(w_down, (expert, part * sub, 0), (1, sub, width))[0]
        grad_moe_own = jnp.where(segment_ids[:, None] > 0, cotangent, jnp.zeros_like(cotangent))
        router = jnp.pad(w_router, ((0, 0), (0, 128 - experts)))
        first.far(own_gu, own_dn, router)
        for m in [0] + ring.links:
            first.core(m)
        blocks = first.blocks()
        w_out = gather(after(out_piece, w_qkv), "shard")
        second = ring.gathering(grad_moe_own)
        second.near(blocks[ring.links[-1]])

        cosine, sine = rotary_tables(length, head_size)
        cosine = jnp.concatenate([cosine, cosine], axis=1)
        sine = jnp.concatenate([-sine, sine], axis=1)
        gains = jnp.stack([query_gain, key_gain])
        order = sorted(pairs, key=lambda m: (-bin(m).count("1"), m))
        singles = ring.singles
        attended = {
            m: attend(blocks[m : m + 2], w_qkv, gains, cosine, sine, length, score_scale) for m in order
        }
        second.far(*[attended[m][1] for m in order])
        for m in [0] + ring.links:
            second.core(m)
        grad_moe = second.blocks()
        w_gu = gather(after(own_gu, w_out, *[attended[m][1] for m in order]), "shard")
        summed = ring.summing()
        for i, m in enumerate(order):
            gate = [attended[k][1] for k in order if k != m] if i == 0 else []
            gate += [grad_moe[ring.links[-1]]] if i == 1 else []
            gate += grad_moe if i == 2 else []
            mixed = after(attended[m][1], *gate) if gate else attended[m][1]
            summed.feed(m, *mix_out(mixed, w_out, length, "mix_out"))
        summed.far()
        near = [summed.near(m) for m in singles]
        attention_out = summed.total()
        w_dn = gather(after(own_dn, *near), "shard")

        hidden = stream + live * attention_out
        second_scale = rms_scale(hidden)
        normed_ffn = (hidden * second_scale * ffn_norm_gain).astype(BF16)
        ffn_all = ring.gather(normed_ffn)

        place = jnp.stack([rep, expert]).astype(jnp.int32)
        entered = {m: expert_in(place, ffn_all[m : m + 2], blocks[m : m + 2], router, w_gu, length, experts) for m in order}
        inner_gated = [entered[m][0] for m in pairs]
        part_dn = weight_grad(inner_gated, grad_moe, hid, 512, "down_grad")
        sum_dn = scatter_sum(part_dn, "shard")
        stepped = {}
        summed = ring.summing()
        for i, m in enumerate(order):
            gate = [summed.core[order[i - 2]]] if i >= 2 else [part_dn]
            if i == len(order) - 1:
                gate += summed.far()
            stepped[m] = expert_back(
                after(place, *gate), grad_moe[m : m + 2], entered[m][1], entered[m][2], w_gu, w_dn, length, reps
            )
            summed.feed(m, *stepped[m][:2])
        near = [summed.near(m) for m in singles]
        grad_gu = [stepped[m][2] for m in pairs]
        grad_gu[0] = after(grad_gu[0], summed.core[order[-1]])
        part_gu = weight_grad(ffn_all, grad_gu, 256, 2 * hid, "up_grad")
        sum_gu = scatter_sum(after(part_gu, sum_dn, *near), "shard")
        grad_ffn = summed.total()
        grad_ffn = after(grad_ffn, part_gu)
        grad_gate = grad_ffn[length : length + 2 * reps, :length]
        grad_gate = jnp.sum(grad_gate.reshape(experts, parts * 2, length), axis=1)
        grad_ffn = grad_ffn[:length]

        logits = dot(normed_ffn, w_router)
        shifted = jnp.exp(logits - jnp.max(logits, axis=-1, keepdims=True))
        chances = shifted / jnp.sum(shifted, axis=-1, keepdims=True)
        picked = jnp.any(expert_ids[:, :, None] == jnp.arange(experts), axis=1)
        grad_chances = jnp.where(picked, grad_gate.T, 0.0)
        grad_logits = chances * (
            grad_chances - jnp.sum(chances * grad_chances, axis=-1, keepdims=True)
        )
        grad_logits = grad_logits.astype(BF16)
        grad_router = dot_tn(normed_ffn, grad_logits)

        grad_result = cotangent.astype(F32)
        grad_normed_ffn = grad_ffn + dot_nt(grad_logits, w_router)
        grad_ffn_gain = jnp.sum(grad_normed_ffn * hidden * second_scale, axis=0)
        grad_hidden = grad_result + norm_back(hidden, second_scale, ffn_norm_gain, grad_normed_ffn)
        grad_attention = ring.gather((live * grad_hidden).astype(BF16))

        moe_sum = ring.summing()
        for m in order:
            moe_sum.feed(m, *mix_out(after(entered[m][0], grad_attention[0]), w_dn, length, "mix_back"))
        backs = {}
        summed = ring.summing()
        backward = list(reversed(order))
        for i, m in enumerate(backward):
            gate = [moe_sum.core[order[min(i, len(order) - 1)]]]
            if i == len(order) - 1:
                gate += moe_sum.far()
            backs[m] = attend_back(
                grad_attention[m : m + 2], blocks[m : m + 2], attended[m][0],
                w_qkv, w_out, after(gains, *gate), cosine, sine, length, score_scale,
            )
            summed.feed(m, *backs[m][:2])
        mixed = [attended[m][1] for m in pairs]
        part_out = weight_grad(mixed, grad_attention, cols, 1024, "out_grad")
        grad_qkv = [backs[m][2] for m in pairs]
        grad_qkv[0] = after(grad_qkv[0], summed.core[backward[-1]])
        part_attention, grad_norm_gain = attention_grad(blocks, grad_qkv, part_out, w_qkv, length, shards, 256)
        grad_norm_gain = grad_norm_gain.reshape(-1) / norm_gain
        moe_last = [moe_sum.near(m) for m in singles]
        far = summed.far(*moe_last)
        normed_last = [summed.near(m) for m in singles]
        moe_out = moe_sum.total()
        grad_normed = summed.total()
        grad_gains = sum(backs[m][3] for m in pairs)
        grad_qgain, grad_kgain = grad_gains[0], grad_gains[1]
        input_grad = grad_hidden + norm_back(stream, first_scale, norm_gain, grad_normed)

        result = hidden + live * moe_out

        sum_attention = scatter_sum(after(part_attention, sum_gu, *moe_last), "shard")
        chops = [sum_dn[:, c : c + 2 * hid] for c in range(0, width, 2 * hid)]
        expert_grads = ring.gathering(jnp.concatenate([sum_gu] + chops))
        expert_grads.near(*far)
        expert_grads.far()
        for m in [0] + ring.links:
            expert_grads.core(m)
        pieces = expert_grads.blocks()

        device = rep ^ jnp.arange(reps, dtype=jnp.int32)
        shapes = ((experts, rows, hidden_total),) * 2 + ((experts, parts * sub, width),)
        all_dn = place_down(pieces, device, rows, sub, width).reshape(shapes[2])
        if sub % 128 == 0:
            units = jnp.stack([lax.div(device, parts), lax.rem(device, parts)], axis=1).reshape(-1)
            all_gate, all_up = place_units(pieces, units, parts, shards, shapes[0], 64)
        else:
            all_gate, all_up = place_hidden(lax.all_gather(sum_gu, "rep"), experts, shards, rows // 4)
        square_sums = jnp.stack(
            [
                jnp.sum(live * stream * stream),
                jnp.sum(live * hidden * hidden),
                jnp.sum(live * result * result),
                jnp.sum(live),
            ]
        )
        small = [grad_norm_gain, grad_ffn_gain, grad_qgain, grad_kgain, grad_router.T.reshape(-1)]
        small.append(jnp.pad(square_sums, (0, 124)))
        small = jnp.concatenate([part.reshape(-1, 128) for part in small])
        count = small.size
        small = total_over_all(small, (("shard", shards),)).reshape(-1)
        wide = 3 * cols
        lines = -(-count // wide)
        small = jnp.pad(small, (0, lines * wide - count)).reshape(lines, wide)
        high = lax.reduce_precision(small, 8, 7)
        low = (small - high).astype(BF16)
        filler = jnp.zeros((-2 * lines % 16, wide), BF16)
        extra = jnp.concatenate([high.astype(BF16), low, filler])
        sum_attention = after(sum_attention, *[expert_grads.held[m] for m in singles], *normed_last, extra)
        last = lax.all_gather(jnp.concatenate([sum_attention[:, :wide], extra]), "rep")
        all_qkv = place_columns(last, rows, 3)
        small = last[:, rows : rows + lines].astype(F32) + last[:, rows + lines : rows + 2 * lines].astype(F32)
        small = jnp.sum(small, axis=0).reshape(-1)
        row_block = lax.rem(device, per_plane) * shards + lax.div(device, per_plane)
        out_piece = after(sum_attention[:, wide:], expert_grads.held[ring.links[-1]])
        out_set = ring.gathering(lax.ppermute(out_piece, ("rep", "shard"), back))
        out_set.near()
        out_set.far(all_gate, all_dn)
        for m in [0] + ring.links:
            out_set.core(m)
        all_out = place_out(out_set.blocks(), row_block, out_rows, (rows, width))
        norm_sum, ffn_sum = small[:width], small[width : 2 * width]
        small = small[2 * width :]
        qgain_sum, kgain_sum = small[:head_size], small[head_size : 2 * head_size]
        router_sum = small[2 * head_size : 2 * head_size + experts * width].reshape(experts, width).T
        stat_sum = small[2 * head_size + experts * width :]
        residual_rms = jnp.sqrt(stat_sum[:3] / (stat_sum[3] * width))
        return (
            result.astype(BF16), input_grad.astype(BF16), norm_sum,
            all_qkv[0], all_qkv[1], all_qkv[2], all_out,
            qgain_sum, kgain_sum, ffn_sum, router_sum,
            all_gate, all_up, all_dn, residual_rms,
        )

    return body


def solution(mesh):
    by_token, by_shard, inner_shard = P(("rep", "shard"), None), P("shard", None), P(None, "shard", None)
    in_specs = (
        by_token, by_token, P(("rep", "shard")), by_token, P(),
        by_shard, by_shard, by_shard, by_shard, P(), P(), P(), P(),
        inner_shard, inner_shard, inner_shard,
    )
    out_specs = (
        by_token, by_token, P(), by_shard, by_shard, by_shard, by_shard, P(), P(), P(), P(),
        inner_shard, inner_shard, inner_shard, P(),
    )
    body = make_body(mesh.shape["rep"], mesh.shape["shard"])
    return jax.shard_map(body, mesh=mesh, in_specs=in_specs, out_specs=out_specs, check_vma=False)
```

```python
import functools

import jax
import jax.numpy as jnp
from jax import lax
from jax.experimental import pallas as pl
from jax.experimental.pallas import tpu as pltpu
from jax.sharding import PartitionSpec as P

EPS = 1e-06
THETA = 10000.0
MASKED = -1e30
F32 = jnp.float32
BF16 = jnp.bfloat16


def rms_scale(field):
    return lax.rsqrt(jnp.mean(field * field, axis=-1, keepdims=True) + EPS)


def norm_back(field, scale, gain, upstream):
    weighted = upstream * gain
    inner = jnp.sum(weighted * field, axis=-1, keepdims=True)
    return scale * weighted - field * scale**3 * inner / field.shape[-1]


def rotary_tables(length, dim):
    half = dim // 2
    frequency = THETA ** (-2.0 * jnp.arange(half, dtype=F32) / dim)
    angles = jnp.arange(length, dtype=F32)[:, None] * frequency[None, :]
    return jnp.cos(angles), jnp.sin(angles)


def rotate(field, cosine, sine):
    half = field.shape[-1] // 2
    first, second = field[..., :half], field[..., half:]
    return jnp.concatenate(
        [first * cosine - second * sine, second * cosine + first * sine], axis=-1
    )


def dot(left, right):
    return jnp.dot(left, right, preferred_element_type=F32)


def dot_nt(left, right):
    return lax.dot_general(left, right, (((1,), (1,)), ((), ())), preferred_element_type=F32)


def dot_tn(left, right):
    return lax.dot_general(left, right, (((0,), (0,)), ((), ())), preferred_element_type=F32)


def after(value, *events):
    return lax.optimization_barrier((value, *events))[0]


def total_over_all(value, sizes):
    for axis, size in sizes:
        bit = 1
        while bit < size:
            value = value + lax.ppermute(value, axis, [(i, i ^ bit) for i in range(size)])
            bit *= 2
    return value


def gather(piece, axis, dim=0):
    return lax.all_gather(piece, axis, axis=dim, tiled=True)


def scatter_sum(whole, axis):
    return lax.psum_scatter(whole, axis, scatter_dimension=0, tiled=True)


IDS = 16


def params(mib=24):
    return pltpu.CompilerParams(vmem_limit_bytes=mib * 2**20)


def whole(array):
    return pl.BlockSpec(array.shape, lambda i: (0,) * len(array.shape), pipeline_mode=pl.Buffered(1))


def cost(flops, arrays):
    moved = sum(a.size * a.dtype.itemsize for a in arrays)
    return pl.CostEstimate(flops=flops, bytes_accessed=moved, transcendentals=0)


def turned(rows):
    rows = jnp.concatenate([rows, jnp.zeros((128 - rows.shape[0], rows.shape[1]), F32)])
    return rows.T


def spin(field, cosine, sine):
    return field * cosine + pltpu.roll(field, field.shape[-1] // 2, 1) * sine


def head_state(raw, ids, gains, cosine, sine, cols, lane, score_scale):
    size = gains.shape[-1]
    query_raw = raw[:, lane : lane + size]
    key_raw = raw[:, cols + lane : cols + lane + size]
    value = raw[:, 2 * cols + lane : 2 * cols + lane + size].astype(BF16)
    query_scale, key_scale = rms_scale(query_raw), rms_scale(key_raw)
    query = spin(query_raw * query_scale * gains[0:1], cosine, sine).astype(BF16)
    key = spin(key_raw * key_scale * gains[1:2], cosine, sine).astype(BF16)
    scores = dot_nt(query, key) * score_scale
    scores = jnp.where(turned(ids)[:, 0:1] == ids[0:1], scores, MASKED)
    exponent = jnp.exp(scores - jnp.max(scores, axis=-1, keepdims=True))
    soft = exponent / jnp.sum(exponent, axis=-1, keepdims=True)
    return query_raw, key_raw, value, query_scale, key_scale, query, key, soft


def attend_kernel(length, score_scale, blk0, blk1, w_qkv, gains, cosine, sine, raw_ref, mixed_ref):
    size = gains.shape[-1]
    cols = w_qkv.shape[1] // 3
    raw = dot(jnp.concatenate([blk0[:length], blk1[:length]]), w_qkv[...])
    raw_ref[...] = raw
    for i, blk in enumerate((blk0, blk1)):
        ids = blk[length : length + IDS, :length].astype(F32)
        mine = raw[i * length : (i + 1) * length]
        for lane in range(0, cols, size):
            state = head_state(mine, ids, gains[...], cosine[...], sine[...], cols, lane, score_scale)
            value, soft = state[2], state[7]
            mixed = dot(soft.astype(BF16), value).astype(BF16)
            mixed_ref[i * length : (i + 1) * length, lane : lane + size] = mixed


def attend(pair, w_qkv, gains, cosine, sine, length, score_scale):
    width, cols = w_qkv.shape[0], w_qkv.shape[1] // 3
    ins = (*pair, w_qkv, gains, cosine, sine)
    specs = [whole(a) for a in ins]
    outs = (
        jax.ShapeDtypeStruct((2 * length, 3 * cols), F32),
        jax.ShapeDtypeStruct((2 * length, cols), BF16),
    )
    return pl.pallas_call(
        functools.partial(attend_kernel, length, score_scale),
        grid=(1,),
        in_specs=specs,
        out_specs=tuple(whole(a) for a in outs),
        out_shape=outs,
        compiler_params=params(),
        cost_estimate=cost(12 * length * width * cols, ins + outs),
        name="attend",
    )(*ins)


def attend_back_kernel(
    length, score_scale, da0, da1, blk0, blk1, raw_ref, w_qkv, w_out, gains, cosine, sine,
    out0, out1, grad_ref, gain_ref,
):
    cols = w_out.shape[0]
    size = gains.shape[-1]
    grad_mixed_all = dot_nt(jnp.concatenate([da0[...], da1[...]]), w_out[...]).astype(BF16)
    qgain = jnp.zeros((1, size), F32)
    kgain = jnp.zeros((1, size), F32)
    for i, (blk, out) in enumerate(((blk0, out0), (blk1, out1))):
        ids = blk[...].astype(F32)
        span = slice(i * length, (i + 1) * length)
        mine = raw_ref[span]
        for lane in range(0, cols, size):
            query_raw, key_raw, value, query_scale, key_scale, query, key, soft = head_state(
                mine, ids, gains[...], cosine[...], sine[...], cols, lane, score_scale
            )
            grad_mixed = grad_mixed_all[span, lane : lane + size]
            grad_value = dot_tn(soft.astype(BF16), grad_mixed).astype(BF16)
            grad_probs = dot_nt(grad_mixed, value)
            row_dot = jnp.sum(soft * grad_probs, axis=-1, keepdims=True)
            grad_scores = (soft * (grad_probs - row_dot)).astype(BF16)
            grad_query = spin(dot(grad_scores, key) * score_scale, cosine[...], -sine[...])
            grad_key = spin(dot_tn(grad_scores, query) * score_scale, cosine[...], -sine[...])
            qgain += jnp.sum(grad_query * query_raw * query_scale, axis=0, keepdims=True)
            kgain += jnp.sum(grad_key * key_raw * key_scale, axis=0, keepdims=True)
            grad_ref[span, lane : lane + size] = norm_back(
                query_raw, query_scale, gains[0:1], grad_query
            ).astype(BF16)
            grad_ref[span, cols + lane : cols + lane + size] = norm_back(
                key_raw, key_scale, gains[1:2], grad_key
            ).astype(BF16)
            grad_ref[span, 2 * cols + lane : 2 * cols + lane + size] = grad_value
        out[...] = dot_nt(grad_ref[span], w_qkv[...]).astype(BF16)
    gain_ref[...] = jnp.concatenate([qgain, kgain, jnp.zeros((6, size), F32)])


def attend_back(pair, ids, raw, w_qkv, w_out, gains, cosine, sine, length, score_scale):
    width, cols = w_qkv.shape[0], w_out.shape[0]
    ins = (*pair, *ids, raw, w_qkv, w_out, gains, cosine, sine)
    outs = (
        jax.ShapeDtypeStruct((length, width), BF16),
        jax.ShapeDtypeStruct((length, width), BF16),
        jax.ShapeDtypeStruct((2 * length, 3 * cols), BF16),
        jax.ShapeDtypeStruct((8, gains.shape[-1]), F32),
    )
    specs = [whole(a) for a in ins]
    for i in (2, 3):
        specs[i] = pl.BlockSpec((IDS, length), lambda i: (length // IDS, 0))
    return pl.pallas_call(
        functools.partial(attend_back_kernel, length, score_scale),
        grid=(1,),
        in_specs=specs,
        out_specs=tuple(whole(a) for a in outs),
        out_shape=outs,
        compiler_params=params(),
        cost_estimate=cost(24 * length * width * cols, ins + outs),
        name="attend_back",
    )(*ins)


def expert_in_kernel(
    length, experts, place, b0, b1, ids0, ids1, w_router, w_gu, gated_ref, inner_ref, factor_ref
):
    hid = w_gu.shape[1] // 2
    expert = place[1]
    field = joined((b0, b1))
    logits = dot(field, w_router[...])
    lane = lax.broadcasted_iota(jnp.int32, logits.shape, 1)
    logits = jnp.where(lane < experts, logits, MASKED)
    chances = jnp.exp(logits - jnp.max(logits, axis=-1, keepdims=True))
    chance = jnp.sum(jnp.where(lane == expert, chances, 0.0), axis=-1, keepdims=True)
    chance = chance / jnp.sum(chances, axis=-1, keepdims=True)
    routes = jnp.concatenate([turned(ids0[...].astype(F32)), turned(ids1[...].astype(F32))])
    wanted = expert.astype(F32)
    chosen = jnp.logical_or(routes[:, 1:2] == wanted, routes[:, 2:3] == wanted)
    gate = jnp.where(chosen, chance, 0.0)
    gate_up = dot(field, w_gu[...])
    gate_pre, up_pre = gate_up[:, :hid], gate_up[:, hid:]
    sigmoid = jax.nn.sigmoid(gate_pre)
    silu = gate_pre * sigmoid
    inner = (silu * up_pre).astype(BF16)
    inner_ref[...] = inner
    gated_ref[...] = (gate * inner.astype(F32)).astype(BF16)
    factor_ref[:, :hid] = gate * up_pre * sigmoid * (1.0 + gate_pre * (1.0 - sigmoid))
    factor_ref[:, hid:] = gate * silu


def expert_in(place, fields, ids, w_router, w_gu, length, experts):
    width, hid = fields[0].shape[1], w_gu.shape[1] // 2
    ins = (place, *fields, *ids, w_router, w_gu)
    outs = (
        jax.ShapeDtypeStruct((2 * length, hid), BF16),
        jax.ShapeDtypeStruct((2 * length, hid), BF16),
        jax.ShapeDtypeStruct((2 * length, 2 * hid), F32),
    )
    specs = [whole(a) for a in ins]
    specs[0] = pl.BlockSpec(memory_space=pltpu.SMEM)
    for i in (3, 4):
        specs[i] = pl.BlockSpec((IDS, length), lambda i: (length // IDS, 0))
    return pl.pallas_call(
        functools.partial(expert_in_kernel, length, experts),
        grid=(1,),
        in_specs=specs,
        out_specs=tuple(whole(a) for a in outs),
        out_shape=outs,
        compiler_params=params(28),
        cost_estimate=cost(8 * length * width * hid, ins + outs),
        name="expert_in",
    )(*ins)


def expert_back_kernel(length, place, c0, c1, inner, factor, w_gu, w_dn, out0, out1, grad_ref):
    hid = w_dn.shape[0]
    rep = place[0]
    grad_inner = dot_nt(joined((c0, c1)), w_dn[...])
    grad_gate = jnp.sum(inner[...].astype(F32) * grad_inner, axis=-1, keepdims=True)
    grad_ref[:, :hid] = (grad_inner * factor[:, :hid]).astype(BF16)
    grad_ref[:, hid:] = (grad_inner * factor[:, hid:]).astype(BF16)
    partial = dot_nt(grad_ref[...], w_gu[...]).astype(BF16)
    grad_gate = jnp.broadcast_to(grad_gate, (2 * length, 128)).T
    extra = out0.shape[0] - length
    row = lax.broadcasted_iota(jnp.int32, (extra, length), 0)
    for i, out in enumerate((out0, out1)):
        out[:length] = partial[i * length : (i + 1) * length]
        whole_grad = grad_gate[:extra, i * length : (i + 1) * length]
        high = whole_grad.astype(BF16).astype(F32)
        parts = jnp.where(row == 2 * rep, high, jnp.where(row == 2 * rep + 1, whole_grad - high, 0.0))
        out[length:, :length] = parts.astype(BF16)
        out[length:, length:] = jnp.zeros((extra, out.shape[1] - length), BF16)


def expert_back(place, grads, inner, factor, w_gu, w_dn, length, reps):
    width, hid = w_dn.shape[1], w_dn.shape[0]
    ins = (place, *grads, inner, factor, w_gu, w_dn)
    tall = length + max(2 * reps, IDS)
    outs = (
        jax.ShapeDtypeStruct((tall, width), BF16),
        jax.ShapeDtypeStruct((tall, width), BF16),
        jax.ShapeDtypeStruct((2 * length, 2 * hid), BF16),
    )
    specs = [whole(a) for a in ins]
    specs[0] = pl.BlockSpec(memory_space=pltpu.SMEM)
    return pl.pallas_call(
        functools.partial(expert_back_kernel, length),
        grid=(1,),
        in_specs=specs,
        out_specs=tuple(whole(a) for a in outs),
        out_shape=outs,
        compiler_params=params(30),
        cost_estimate=cost(12 * length * width * hid, ins + outs),
        name="expert_back",
    )(*ins)


def mix_out_kernel(length, mixed, w_out, out0, out1):
    both = dot(mixed[...], w_out[...]).astype(BF16)
    out0[...] = both[:length]
    out1[...] = both[length:]


def mix_out(mixed, w_out, length, name):
    out = jax.ShapeDtypeStruct((length, w_out.shape[1]), BF16)
    ins = (mixed, w_out)
    return pl.pallas_call(
        functools.partial(mix_out_kernel, length),
        grid=(1,),
        in_specs=[whole(a) for a in ins],
        out_specs=(whole(out), whole(out)),
        out_shape=(out, out),
        compiler_params=params(16),
        cost_estimate=cost(4 * length * w_out.size, (*ins, out, out)),
        name=name,
    )(*ins)


def joined(refs):
    return jnp.concatenate([ref[...] for ref in refs])


def weight_grad_kernel(count, *refs):
    refs[-1][...] = dot_tn(joined(refs[:count]), joined(refs[count:-1])).astype(BF16)


def weight_grad(left, right, tile, wide, name):
    out = jax.ShapeDtypeStruct((left[0].shape[1], right[0].shape[1]), BF16)
    ins = (*left, *right)
    rows_step, cols_step = int(tile < out.shape[0]), int(wide < out.shape[1])
    return pl.pallas_call(
        functools.partial(weight_grad_kernel, len(left)),
        grid=(out.shape[0] // tile if rows_step else out.shape[1] // wide,),
        in_specs=[pl.BlockSpec((a.shape[0], tile), lambda i: (0, i * rows_step)) for a in left]
        + [pl.BlockSpec((a.shape[0], wide), lambda i: (0, i * cols_step)) for a in right],
        out_specs=pl.BlockSpec((tile, wide), lambda i: (i * rows_step, i * cols_step)),
        out_shape=out,
        compiler_params=params(),
        cost_estimate=cost(2 * left[0].shape[0] * len(left) * out.size, (*ins, out)),
        name=name,
    )(*ins)


def attention_grad_kernel(count, out_rows, *refs):
    left, right, (extra, weight, out, gain) = refs[:count], refs[count:-4], refs[-4:]
    tile, columns = left[0].shape[1], right[0].shape[1]
    cols = out.shape[1] - columns
    grad = dot_tn(joined(left), joined(right))
    out[:, :columns] = grad.astype(BF16)
    gain[...] = jnp.sum(grad * weight[...].astype(F32), axis=-1, keepdims=True)
    chunks = extra.shape[1] // cols
    for k in range(tile // out_rows):
        place = pl.program_id(0) * (tile // out_rows) + k
        row = pl.multiple_of(lax.div(place, chunks) * out_rows, out_rows)
        lane = pl.multiple_of(lax.rem(place, chunks) * cols, cols)
        out[k * out_rows : (k + 1) * out_rows, columns:] = extra[pl.ds(row, out_rows), pl.ds(lane, cols)]


def attention_grad(left, right, extra, weight, length, shards, tile):
    width, columns, cols = left[0].shape[1], right[0].shape[1], extra.shape[0]
    outs = (jax.ShapeDtypeStruct((width, columns + cols), BF16), jax.ShapeDtypeStruct((width, 1), F32))
    return pl.pallas_call(
        functools.partial(attention_grad_kernel, len(left), cols // shards),
        grid=(width // tile,),
        in_specs=[pl.BlockSpec((length, tile), lambda i: (0, i)) for _ in left]
        + [pl.BlockSpec(a.shape, lambda i: (0, 0)) for a in (*right, extra)]
        + [pl.BlockSpec((tile, columns), lambda i: (i, 0))],
        out_specs=(
            pl.BlockSpec((tile, columns + cols), lambda i: (i, 0)),
            pl.BlockSpec((tile, 1), lambda i: (i, 0)),
        ),
        out_shape=outs,
        compiler_params=params(),
        cost_estimate=cost(2 * length * len(left) * width * columns, (*left, *right, *outs)),
        name="attention_grad",
    )(*left, *right, extra, weight)


def own_columns_kernel(place, query, key, value, out):
    cols = query.shape[1]
    for i, ref in enumerate((query, key, value)):
        out[:, i * cols : (i + 1) * cols] = ref[...]


def own_columns(weights, rep, cols):
    rows = weights[0].shape[0]
    return pl.pallas_call(
        own_columns_kernel,
        grid_spec=pltpu.PrefetchScalarGridSpec(
            num_scalar_prefetch=1,
            grid=(1,),
            in_specs=[pl.BlockSpec((rows, cols), lambda i, place: (0, place[0]))] * len(weights),
            out_specs=pl.BlockSpec((rows, len(weights) * cols), lambda i, place: (0, 0)),
        ),
        out_shape=jax.ShapeDtypeStruct((rows, len(weights) * cols), BF16),
        compiler_params=params(),
        name="own_columns",
    )(rep.reshape(1), *weights)


def own_expert_kernel(place, gate, up, down, gu, dn):
    step = pl.program_id(0)
    sub = gate.shape[2]
    for i, ref in enumerate((gate, up)):
        gu[:, pl.ds(pl.multiple_of(i * gu.shape[1] // 2 + step * sub, 128), sub)] = ref[0]

    @pl.when(step == 0)
    def _():
        dn[...] = down[0]


def own_expert(gate, up, down, table, parts, sub):
    _, rows, wide = gate.shape
    width = down.shape[2]
    hid = wide // parts
    spec = pl.BlockSpec((1, rows, sub), lambda z, place: (place[0], 0, z * parts + place[1]))
    return pl.pallas_call(
        own_expert_kernel,
        grid_spec=pltpu.PrefetchScalarGridSpec(
            num_scalar_prefetch=1,
            grid=(hid // sub,),
            in_specs=[spec, spec, pl.BlockSpec((1, sub, width), lambda z, place: (place[0], place[1], 0))],
            out_specs=(
                pl.BlockSpec((rows, 2 * hid), lambda z, place: (0, 0)),
                pl.BlockSpec((sub, width), lambda z, place: (0, 0)),
            ),
        ),
        out_shape=(jax.ShapeDtypeStruct((rows, 2 * hid), BF16), jax.ShapeDtypeStruct((sub, width), BF16)),
        compiler_params=params(),
        name="own_expert",
    )(table, gate, up, down)


def place_out_kernel(rows, place, *refs):
    out = refs[-1]
    cols = refs[0].shape[1]
    for m, source in enumerate(refs[:-1]):
        row = pl.multiple_of(place[m] * rows, rows)
        for c in range(out.shape[1] // cols):
            out[pl.ds(row, rows), c * cols : (c + 1) * cols] = source[c * rows : (c + 1) * rows].astype(F32)


def place_out(pieces, table, rows, shape):
    return pl.pallas_call(
        functools.partial(place_out_kernel, rows),
        grid_spec=pltpu.PrefetchScalarGridSpec(
            num_scalar_prefetch=1,
            grid=(1,),
            in_specs=[pl.BlockSpec(a.shape, lambda i, place: (0, 0)) for a in pieces],
            out_specs=pl.BlockSpec(shape, lambda i, place: (0, 0)),
        ),
        out_shape=jax.ShapeDtypeStruct(shape, F32),
        compiler_params=params(),
        cost_estimate=cost(0, [jax.ShapeDtypeStruct((2, *shape), F32)]),
        name="place_out",
    )(table, *pieces)


def place_units_kernel(parts, shards, place, *refs):
    sources, (out_gate, out_up) = refs[:-2], refs[-2:]
    sub = sources[0].shape[1] // 2 // shards
    for m, source in enumerate(sources):
        expert, part = place[2 * m], place[2 * m + 1]
        for i, out in enumerate((out_gate, out_up)):
            for z in range(shards):
                lane = pl.multiple_of((z * parts + part) * sub, 128)
                at = (i * shards + z) * sub
                out[expert, :, pl.ds(lane, sub)] = source[:, at : at + sub].astype(F32)


def place_units(pieces, table, parts, shards, shape, tile):
    wide = pieces[0].shape[1]
    return pl.pallas_call(
        functools.partial(place_units_kernel, parts, shards),
        grid_spec=pltpu.PrefetchScalarGridSpec(
            num_scalar_prefetch=1,
            grid=(shape[1] // tile,),
            in_specs=[pl.BlockSpec((tile, wide), lambda t, place: (t, 0)) for _ in pieces],
            out_specs=[pl.BlockSpec((shape[0], tile, shape[2]), lambda t, place: (0, t, 0))] * 2,
        ),
        out_shape=[jax.ShapeDtypeStruct(shape, F32)] * 2,
        compiler_params=params(),
        cost_estimate=cost(0, [jax.ShapeDtypeStruct((4, *shape), F32)]),
        name="place_units",
    )(table, *pieces)


def place_down_kernel(place, *refs):
    sub = refs[0].shape[0]
    for m, source in enumerate(refs[:-1]):
        refs[-1][pl.ds(pl.multiple_of(place[m] * sub, sub), sub), :] = source[...].astype(F32)


def place_down(pieces, table, rows, sub, width):
    wide = pieces[0].shape[1]
    return pl.pallas_call(
        place_down_kernel,
        grid_spec=pltpu.PrefetchScalarGridSpec(
            num_scalar_prefetch=1,
            grid=(width // wide,),
            in_specs=[pl.BlockSpec((sub, wide), lambda c, place: (rows // sub + c, 0)) for _ in pieces],
            out_specs=pl.BlockSpec((len(pieces) * sub, wide), lambda c, place: (0, c)),
        ),
        out_shape=jax.ShapeDtypeStruct((len(pieces) * sub, width), F32),
        compiler_params=params(),
        cost_estimate=cost(0, [jax.ShapeDtypeStruct((len(pieces) * sub, 2 * width), F32)]),
        name="place_down",
    )(table, *pieces)


def place_columns_kernel(source, *outs):
    cols = outs[0].shape[1]
    for i, out in enumerate(outs):
        out[...] = source[0, :, i * cols : (i + 1) * cols].astype(F32)


def place_columns(source, rows, count):
    reps, _, wide = source.shape
    cols = wide // count
    return pl.pallas_call(
        place_columns_kernel,
        grid=(reps,),
        in_specs=[pl.BlockSpec((1, rows, wide), lambda r: (r, 0, 0))],
        out_specs=[pl.BlockSpec((rows, cols), lambda r: (0, r)) for _ in range(count)],
        out_shape=[jax.ShapeDtypeStruct((rows, reps * cols), F32) for _ in range(count)],
        compiler_params=params(),
        name="place_columns",
    )(source)


def place_hidden_kernel(parts, shards, sub, source, *outs):
    hid = shards * sub
    for i, out in enumerate(outs):
        for z in range(shards):
            for p in range(parts):
                lane = i * hid + z * sub
                out[0, :, (z * parts + p) * sub : (z * parts + p + 1) * sub] = source[
                    p, :, lane : lane + sub
                ].astype(F32)


def place_hidden(source, experts, shards, tile):
    reps, rows, wide = source.shape
    parts = reps // experts
    full = parts * wide // 2
    return pl.pallas_call(
        functools.partial(place_hidden_kernel, parts, shards, wide // 2 // shards),
        grid=(experts, rows // tile),
        in_specs=[pl.BlockSpec((parts, tile, wide), lambda e, t: (e, t, 0))],
        out_specs=[pl.BlockSpec((1, tile, full), lambda e, t: (e, t, 0)) for _ in range(2)],
        out_shape=[jax.ShapeDtypeStruct((experts, rows, full), F32) for _ in range(2)],
        compiler_params=params(),
        name="place_hidden",
    )(source)


class Ring:
    def __init__(self, reps):
        self.reps = reps
        self.links = [m for m in range(2, reps, 2)]
        self.links.sort(key=lambda m: (bin(m).count("1"), m))
        self.singles = [m for m in self.links if m & (m - 1) == 0]

    def swap(self, piece, bit):
        return lax.ppermute(piece, "rep", [(i, i ^ bit) for i in range(self.reps)])

    @staticmethod
    def hops(m):
        return 1 << (m.bit_length() - 1), m & -m

    def gathering(self, block):
        return RingGather(self, block)

    def gather(self, block):
        whole_set = RingGather(self, block)
        whole_set.near()
        whole_set.far()
        for m in [0] + self.links:
            whole_set.core(m)
        return whole_set.blocks()

    def summing(self):
        return RingSum(self)


class RingGather:
    def __init__(self, ring, block):
        self.ring = ring
        self.half = max(block.shape[0] // 32 * 16, 8)
        self.held = {0: block}

    def near(self, *gate):
        block = after(self.held[0], *gate) if gate else self.held[0]
        for m in self.ring.singles:
            self.held[m] = self.ring.swap(block, m)

    def far(self, *gate):
        for m in self.ring.links:
            high, low = self.ring.hops(m)
            if high == low:
                continue
            first, second = self.held[m ^ high][: self.half], self.held[m ^ low][self.half :]
            if gate:
                first, second = after((first, second), *gate)
            self.held[m] = jnp.concatenate([self.ring.swap(first, high), self.ring.swap(second, low)])

    def core(self, m, *gate):
        block = after(self.held[m], *gate) if gate else self.held[m]
        self.held[m ^ 1] = self.ring.swap(block, 1)

    def pair(self, m):
        return [self.held[m], self.held[m ^ 1]]

    def blocks(self):
        return [self.held[m] for m in range(self.ring.reps)]


class RingSum:
    def __init__(self, ring):
        self.ring = ring
        self.held = {}
        self.core = {}

    def feed(self, m, own, other):
        self.half = max(own.shape[0] // 32 * 16, 8)
        got = self.core[m] = self.ring.swap(other, 1)
        parts = (slice(None, self.half), slice(self.half, None))
        self.held[m] = [own[part].astype(F32) + got[part].astype(F32) for part in parts]

    def far(self, *gate):
        events = []
        for m in reversed(self.ring.links):
            high, low = self.ring.hops(m)
            if high == low:
                continue
            for part, bit in ((0, high), (1, low)):
                piece = self.held[m][part].astype(BF16)
                got = self.ring.swap(after(piece, *gate) if gate else piece, bit)
                self.held[m ^ bit][part] = self.held[m ^ bit][part] + got.astype(F32)
                events.append(got)
        return events

    def near(self, m, *gate):
        piece = jnp.concatenate(self.held[m]).astype(BF16)
        got = self.ring.swap(after(piece, *gate) if gate else piece, m)
        for part, rows in ((0, slice(None, self.half)), (1, slice(self.half, None))):
            self.held[0][part] = self.held[0][part] + got[rows].astype(F32)
        return got

    def total(self):
        return jnp.concatenate(self.held[0])


def make_body(reps, shards):
    ring = Ring(reps)

    def body(
        tokens, cotangent, segment_ids, expert_ids, norm_gain, w_query, w_key, w_value, w_output,
        query_gain, key_gain, ffn_norm_gain, w_router, w_gate, w_up, w_down,
    ):
        length, width = tokens.shape
        head_size = query_gain.shape[0]
        head_count = width // head_size
        experts = w_gate.shape[0]
        hidden_total = w_gate.shape[2]
        heads = head_count // reps
        cols = heads * head_size
        parts = reps // experts
        sub = hidden_total // shards // parts
        hid = sub * shards
        rows = width // shards
        total = reps * length
        per_plane = reps // shards
        out_rows = cols // shards
        score_scale = head_size ** (-0.5)

        rep = lax.axis_index("rep")
        expert, part = lax.div(rep, parts), lax.rem(rep, parts)

        def hidden_columns(weight):
            own = lax.dynamic_slice(weight, (expert, 0, 0), (1, rows, hidden_total))
            own = own.reshape(rows, shards, parts, sub)
            return lax.dynamic_slice(own, (0, 0, part, 0), (rows, shards, 1, sub)).reshape(rows, hid)

        there = [
            (src_rep * shards + src, (src * per_plane + src_rep % per_plane) * shards + src_rep // per_plane)
            for src_rep in range(reps)
            for src in range(shards)
        ]
        back = [(target, source) for source, target in there]
        own_rows = lax.dynamic_slice(w_output, (lax.rem(rep, per_plane) * cols, 0), (cols, width))
        own_rows = jnp.where(lax.axis_index("shard") == lax.div(rep, per_plane), own_rows, jnp.zeros_like(own_rows))
        w_qkv = gather(own_columns((w_query, w_key, w_value), rep, cols), "shard")

        stream = tokens.astype(F32)
        live = (segment_ids > 0).astype(F32)[:, None]
        first_scale = rms_scale(stream)
        normed = (stream * first_scale * norm_gain).astype(BF16)
        ids = jnp.concatenate([segment_ids[None], expert_ids.T]).astype(BF16)
        ids = jnp.pad(ids, ((0, IDS - ids.shape[0]), (0, width - length)))
        first = ring.gathering(jnp.concatenate([normed, ids]))
        first.near()
        pairs = range(0, reps, 2)

        unit = jnp.stack([expert, part]).astype(jnp.int32)
        if sub % 128 == 0:
            own_gu, own_dn = own_expert(w_gate, w_up, w_down, unit, parts, sub)
        else:
            own_gu = jnp.concatenate([hidden_columns(w_gate), hidden_columns(w_up)], 1)
            own_dn = lax.dynamic_slice(w_down, (expert, part * sub, 0), (1, sub, width))[0]
        grad_moe_own = jnp.where(segment_ids[:, None] > 0, cotangent, jnp.zeros_like(cotangent))
        router = jnp.pad(w_router, ((0, 0), (0, 128 - experts)))
        first.far(own_gu, own_dn, router)
        for m in [0] + ring.links:
            first.core(m)
        blocks = first.blocks()
        w_out = lax.psum(after(own_rows, w_qkv), "shard")
        second = ring.gathering(grad_moe_own)
        second.near(w_qkv)

        cosine, sine = rotary_tables(length, head_size)
        cosine = jnp.concatenate([cosine, cosine], axis=1)
        sine = jnp.concatenate([-sine, sine], axis=1)
        gains = jnp.stack([query_gain, key_gain])
        order = sorted(pairs, key=lambda m: (-bin(m).count("1"), m))
        singles = ring.singles
        attended = {
            m: attend(blocks[m : m + 2], w_qkv, gains, cosine, sine, length, score_scale) for m in order
        }
        second.far(*[attended[m][1] for m in order])
        for m in [0] + ring.links:
            second.core(m)
        grad_moe = second.blocks()
        w_gu = gather(after(own_gu, w_out, *[attended[m][1] for m in order]), "shard")
        summed = ring.summing()
        for i, m in enumerate(order):
            gate = [attended[k][1] for k in order if k != m] if i == 0 else []
            gate += [grad_moe[ring.links[-1]]] if i == 1 else []
            gate += grad_moe if i == 2 else []
            mixed = after(attended[m][1], *gate) if gate else attended[m][1]
            summed.feed(m, *mix_out(mixed, w_out, length, "mix_out"))
        summed.far()
        near = [summed.near(m) for m in singles]
        attention_out = summed.total()
        w_dn = gather(after(own_dn, *near), "shard")

        hidden = stream + live * attention_out
        second_scale = rms_scale(hidden)
        normed_ffn = (hidden * second_scale * ffn_norm_gain).astype(BF16)
        ffn_all = ring.gather(normed_ffn)

        place = jnp.stack([rep, expert]).astype(jnp.int32)
        entered = {m: expert_in(place, ffn_all[m : m + 2], blocks[m : m + 2], router, w_gu, length, experts) for m in order}
        inner_gated = [entered[m][0] for m in pairs]
        part_dn = weight_grad(inner_gated, grad_moe, hid, 512, "down_grad")
        sum_dn = scatter_sum(part_dn, "shard")
        stepped = {}
        summed = ring.summing()
        for i, m in enumerate(order):
            gate = [summed.core[order[i - 2]]] if i >= 2 else [part_dn]
            if i == len(order) - 1:
                gate += summed.far()
            stepped[m] = expert_back(
                after(place, *gate), grad_moe[m : m + 2], entered[m][1], entered[m][2], w_gu, w_dn, length, reps
            )
            summed.feed(m, *stepped[m][:2])
        near = [summed.near(m) for m in singles]
        grad_gu = [stepped[m][2] for m in pairs]
        grad_gu[0] = after(grad_gu[0], summed.core[order[-1]])
        part_gu = weight_grad(ffn_all, grad_gu, 256, 2 * hid, "up_grad")
        sum_gu = scatter_sum(after(part_gu, sum_dn, *near), "shard")
        grad_ffn = summed.total()
        grad_ffn = after(grad_ffn, part_gu)
        grad_gate = grad_ffn[length : length + 2 * reps, :length]
        grad_gate = jnp.sum(grad_gate.reshape(experts, parts * 2, length), axis=1)
        grad_ffn = grad_ffn[:length]

        logits = dot(normed_ffn, w_router)
        shifted = jnp.exp(logits - jnp.max(logits, axis=-1, keepdims=True))
        chances = shifted / jnp.sum(shifted, axis=-1, keepdims=True)
        picked = jnp.any(expert_ids[:, :, None] == jnp.arange(experts), axis=1)
        grad_chances = jnp.where(picked, grad_gate.T, 0.0)
        grad_logits = chances * (
            grad_chances - jnp.sum(chances * grad_chances, axis=-1, keepdims=True)
        )
        grad_logits = grad_logits.astype(BF16)
        grad_router = dot_tn(normed_ffn, grad_logits)

        grad_result = cotangent.astype(F32)
        grad_normed_ffn = grad_ffn + dot_nt(grad_logits, w_router)
        grad_ffn_gain = jnp.sum(grad_normed_ffn * hidden * second_scale, axis=0)
        grad_hidden = grad_result + norm_back(hidden, second_scale, ffn_norm_gain, grad_normed_ffn)
        grad_attention = ring.gather((live * grad_hidden).astype(BF16))

        moe_sum = ring.summing()
        for m in order:
            moe_sum.feed(m, *mix_out(after(entered[m][0], grad_attention[0]), w_dn, length, "mix_back"))
        backs = {}
        summed = ring.summing()
        backward = list(reversed(order))
        for i, m in enumerate(backward):
            gate = [moe_sum.core[order[min(i, len(order) - 1)]]]
            if i == len(order) - 1:
                gate += moe_sum.far()
            backs[m] = attend_back(
                grad_attention[m : m + 2], blocks[m : m + 2], attended[m][0],
                w_qkv, w_out, after(gains, *gate), cosine, sine, length, score_scale,
            )
            summed.feed(m, *backs[m][:2])
        mixed = [attended[m][1] for m in pairs]
        part_out = weight_grad(mixed, grad_attention, cols, 1024, "out_grad")
        grad_qkv = [backs[m][2] for m in pairs]
        grad_qkv[0] = after(grad_qkv[0], summed.core[backward[-1]])
        part_attention, grad_norm_gain = attention_grad(blocks, grad_qkv, part_out, w_qkv, length, shards, 256)
        grad_norm_gain = grad_norm_gain.reshape(-1) / norm_gain
        moe_last = [moe_sum.near(m) for m in singles]
        far = summed.far(*moe_last)
        normed_last = [summed.near(m) for m in singles]
        moe_out = moe_sum.total()
        grad_normed = summed.total()
        grad_gains = sum(backs[m][3] for m in pairs)
        grad_qgain, grad_kgain = grad_gains[0], grad_gains[1]
        input_grad = grad_hidden + norm_back(stream, first_scale, norm_gain, grad_normed)

        result = hidden + live * moe_out

        sum_attention = scatter_sum(after(part_attention, sum_gu, *moe_last), "shard")
        chops = [sum_dn[:, c : c + 2 * hid] for c in range(0, width, 2 * hid)]
        expert_grads = ring.gathering(jnp.concatenate([sum_gu] + chops))
        expert_grads.near(*far)
        expert_grads.far()
        for m in [0] + ring.links:
            expert_grads.core(m)
        pieces = expert_grads.blocks()

        device = rep ^ jnp.arange(reps, dtype=jnp.int32)
        shapes = ((experts, rows, hidden_total),) * 2 + ((experts, parts * sub, width),)
        all_dn = place_down(pieces, device, rows, sub, width).reshape(shapes[2])
        if sub % 128 == 0:
            units = jnp.stack([lax.div(device, parts), lax.rem(device, parts)], axis=1).reshape(-1)
            all_gate, all_up = place_units(pieces, units, parts, shards, shapes[0], 64)
        else:
            all_gate, all_up = place_hidden(lax.all_gather(sum_gu, "rep"), experts, shards, rows // 4)
        square_sums = jnp.stack(
            [
                jnp.sum(live * stream * stream),
                jnp.sum(live * hidden * hidden),
                jnp.sum(live * result * result),
                jnp.sum(live),
            ]
        )
        small = [grad_norm_gain, grad_ffn_gain, grad_qgain, grad_kgain, grad_router.T.reshape(-1)]
        small.append(jnp.pad(square_sums, (0, 124)))
        small = jnp.concatenate([part.reshape(-1, 128) for part in small])
        count = small.size
        small = total_over_all(small, (("shard", shards),)).reshape(-1)
        wide = 3 * cols
        lines = -(-count // wide)
        small = jnp.pad(small, (0, lines * wide - count)).reshape(lines, wide)
        high = lax.reduce_precision(small, 8, 7)
        low = (small - high).astype(BF16)
        filler = jnp.zeros((-2 * lines % 16, wide), BF16)
        extra = jnp.concatenate([high.astype(BF16), low, filler])
        sum_attention = after(sum_attention, *[expert_grads.held[m] for m in singles], *normed_last, extra)
        last = lax.all_gather(jnp.concatenate([sum_attention[:, :wide], extra]), "rep")
        all_qkv = place_columns(last, rows, 3)
        small = last[:, rows : rows + lines].astype(F32) + last[:, rows + lines : rows + 2 * lines].astype(F32)
        small = jnp.sum(small, axis=0).reshape(-1)
        row_block = lax.rem(device, per_plane) * shards + lax.div(device, per_plane)
        out_piece = after(sum_attention[:, wide:], expert_grads.held[ring.links[-1]])
        out_set = ring.gathering(lax.ppermute(out_piece, ("rep", "shard"), back))
        out_set.near()
        out_set.far(all_gate, all_dn)
        for m in [0] + ring.links:
            out_set.core(m)
        all_out = place_out(out_set.blocks(), row_block, out_rows, (rows, width))
        norm_sum, ffn_sum = small[:width], small[width : 2 * width]
        small = small[2 * width :]
        qgain_sum, kgain_sum = small[:head_size], small[head_size : 2 * head_size]
        router_sum = small[2 * head_size : 2 * head_size + experts * width].reshape(experts, width).T
        stat_sum = small[2 * head_size + experts * width :]
        residual_rms = jnp.sqrt(stat_sum[:3] / (stat_sum[3] * width))
        return (
            result.astype(BF16), input_grad.astype(BF16), norm_sum,
            all_qkv[0], all_qkv[1], all_qkv[2], all_out,
            qgain_sum, kgain_sum, ffn_sum, router_sum,
            all_gate, all_up, all_dn, residual_rms,
        )

    return body


def solution(mesh):
    by_token, by_shard, inner_shard = P(("rep", "shard"), None), P("shard", None), P(None, "shard", None)
    in_specs = (
        by_token, by_token, P(("rep", "shard")), by_token, P(),
        by_shard, by_shard, by_shard, by_shard, P(), P(), P(), P(),
        inner_shard, inner_shard, inner_shard,
    )
    out_specs = (
        by_token, by_token, P(), by_shard, by_shard, by_shard, by_shard, P(), P(), P(), P(),
        inner_shard, inner_shard, inner_shard, P(),
    )
    body = make_body(mesh.shape["rep"], mesh.shape["shard"])
    return jax.shard_map(body, mesh=mesh, in_specs=in_specs, out_specs=out_specs, check_vma=False)
```
